768 devices in a mesh: grp: 48 (over z, x), dev: 16 (over y, core).
Axes of the slice: x: 4, y: 8, z: 12, core: 2. Of those that a mesh axis runs over, the one named last changes fastest.
Arguments:
- block_states: float32 [6144, 5, 4096], P(('grp', 'dev')), may hold values from -2 to 10.5, as said below
- dest_dev: int32 [6144], P('grp'), may hold values from -1 to 15, as said below
- dest_slot: int32 [6144], P('grp'), may hold values from 0 to 3, as said below
- neighbours: int32 [2, 3072], P(None, 'grp'), may hold values from -1 to 63, as said below
- coarse_map: int32 [16, 192], P('dev'), may hold values from 0 to 191, each once within a row
Outputs:
- advanced: float32 [3072, 5, 4096], P(('grp', 'dev'))
- registers: float32 [768, 5, 256], P(('grp', 'dev'))
The draws below stay inside these ranges and needn't reach their ends.
Inputs may be any that keep to these rules, and one draw needn't show every extreme that they name: `block_states`: every slot holds a physical state: density 0.5 to 2, each velocity component -1 to 1, pressure 0.3 to 3. `dest_dev`: each pair of a receiving device index and a slot 0 .. 3 of a group gets exactly one patch; a device keeps its own patches or sends at most one patch to each of the next 3 device indices of its group (counted modulo 16) and to no other. `dest_slot`: see dest_dev. Index dev * 4 + slot within the group; neighbours are mutual (neighbours[1, a] = b exactly when neighbours[0, b] = a, within a group), a neighbour's index differs from the patch's own by at most 3, and -1 marks a domain boundary. `coarse_map`: for each device index a permutation: value m names register m // 4 in the group order, quadrant m % 4.
All inputs are finite; a program needn't handle non-finite values.
Results may differ from the reference program's by a relative error of at most 0.0003.
Values sent between devices are 32-bit elements; how exact they have to be, the bound alone decides.
A program may use at most 32 MiB of HBM per device.

```python
import math
import jax
import jax.numpy as jnp
from jax import lax

SIDE_LENGTH = 16
STATE_VARIABLES = 5
DEVICE_PATCHES = 4
P_DEV = 8
SLOTS_IN = 6144
BLOCK_NUMBER = 3072
REGS = 768
N_GRP = 48
N_DEV = 16


def rebalance_plan(key):
    base_key = jax.random.fold_in(key, 11)
    key_bits = jax.random.fold_in(base_key, 1)
    key_slots = jax.random.fold_in(base_key, 2)
    offsets = jnp.broadcast_to(jnp.arange(1, DEVICE_PATCHES, dtype=jnp.int32), (N_GRP, DEVICE_PATCHES - 1))
    bits = jax.random.randint(key_bits, (N_GRP, N_DEV, DEVICE_PATCHES - 1), 0, 2)
    sources = jnp.arange(N_DEV, dtype=jnp.int32)[None, :, None]
    receivers = ((sources + offsets[:, None, :]) % N_DEV).astype(jnp.int32)
    sending = jnp.take_along_axis(bits, receivers, axis=1)
    staying = jnp.concatenate([jnp.ones((N_GRP, N_DEV, 1), jnp.int32), 1 - bits], axis=2)
    stay_dev = jnp.where(staying == 1, jnp.broadcast_to(sources, staying.shape), -1)
    send_dev = jnp.where(sending == 1, receivers, -1)
    cand_dev = jnp.concatenate([stay_dev, send_dev, -jnp.ones((N_GRP, N_DEV, 1), jnp.int32)], axis=2).astype(jnp.int32)
    stay_slot = jnp.broadcast_to(jnp.arange(DEVICE_PATCHES, dtype=jnp.int32), (N_GRP, N_DEV, DEVICE_PATCHES))
    send_slot = jnp.broadcast_to(jnp.arange(1, DEVICE_PATCHES, dtype=jnp.int32), (N_GRP, N_DEV, DEVICE_PATCHES - 1))
    cand_slot = jnp.concatenate([stay_slot, send_slot, jnp.zeros((N_GRP, N_DEV, 1), jnp.int32)], axis=2)
    cand_slot = jnp.where(cand_dev >= 0, cand_slot, 0)
    order = jax.vmap(lambda subkey: jax.random.permutation(subkey, 2 * DEVICE_PATCHES))(jax.random.split(key_slots, N_GRP * N_DEV))
    order = order.reshape(N_GRP, N_DEV, 2 * DEVICE_PATCHES).astype(jnp.int32)
    dest_dev = jnp.take_along_axis(cand_dev, order, axis=2).reshape(-1).astype(jnp.int32)
    dest_slot = jnp.take_along_axis(cand_slot, order, axis=2).reshape(-1).astype(jnp.int32)
    return (dest_dev, dest_slot)


def draw_dest_dev(key, part):
    return rebalance_plan(key)[0]


def draw_dest_slot(key, part):
    return rebalance_plan(key)[1]


def draw_neighbours(key, part):
    key_swap, key_cut = jax.random.split(jax.random.fold_in(key, 37))
    group_size = N_DEV * DEVICE_PATCHES
    position = jnp.arange(group_size, dtype=jnp.int32)
    swapping = jax.random.randint(key_swap, (N_GRP, group_size // 2, 1), 0, 2)
    paired = position.reshape(1, group_size // 2, 2)
    flipped = paired[:, :, ::-1]
    order = jnp.where(swapping == 1, flipped, paired).reshape(N_GRP, group_size).astype(jnp.int32)
    cutting = jax.random.randint(key_cut, (N_GRP, group_size - 1), 0, 8) == 0
    cutting = cutting & (jnp.arange(group_size - 1, dtype=jnp.int32)[None, :] < group_size - 4)
    lower_pos = jnp.concatenate([-jnp.ones((N_GRP, 1), jnp.int32), jnp.where(cutting, -1, order[:, :-1])], axis=1)
    upper_pos = jnp.concatenate([jnp.where(cutting, -1, order[:, 1:]), -jnp.ones((N_GRP, 1), jnp.int32)], axis=1)
    lower = jnp.take_along_axis(lower_pos, order, axis=1).reshape(-1)
    upper = jnp.take_along_axis(upper_pos, order, axis=1).reshape(-1)
    return jnp.stack([lower, upper], axis=0).astype(jnp.int32)


def draw_block_states(key, part):
    keys = jax.random.split(jax.random.fold_in(key, 23), 7)
    shape = (SLOTS_IN, SIDE_LENGTH ** 3)
    density = jax.random.uniform(keys[0], shape, jnp.float32, 0.5, 2.0)
    vel_x = jax.random.uniform(keys[1], shape, jnp.float32, -1.0, 1.0)
    vel_y = jax.random.uniform(keys[2], shape, jnp.float32, -1.0, 1.0)
    vel_z = jax.random.uniform(keys[6], shape, jnp.float32, -1.0, 1.0)
    pressure = jnp.exp(jax.random.uniform(keys[3], shape, jnp.float32, math.log(0.3), math.log(3.0)))
    energy = pressure / 0.4 + 0.5 * density * (vel_x * vel_x + vel_y * vel_y + vel_z * vel_z)
    stacked = jnp.stack([density, density * vel_x, density * vel_y, density * vel_z, energy], axis=1)
    return stacked.astype(jnp.float32)


def setup_inputs(seed: int = 0) -> dict:
    seeds = jax.random.split(jax.random.key(seed), 6)
    return {
        "block_states": draw_block_states(jax.random.fold_in(seeds[5], 71), 0),
        "dest_dev": draw_dest_dev(jax.random.fold_in(seeds[5], 71), 0),
        "dest_slot": draw_dest_slot(jax.random.fold_in(seeds[5], 71), 0),
        "neighbours": draw_neighbours(jax.random.fold_in(seeds[5], 71), 0),
        "coarse_map": jax.vmap(lambda own: jax.random.permutation(own, N_GRP * DEVICE_PATCHES))(jax.random.split(seeds[4], N_DEV)).reshape((N_DEV, N_GRP * DEVICE_PATCHES)).astype(jnp.int32),
    }


GAMMA = 1.4
COURANT = 0.2

def primitives(conserved):
    density = conserved[..., 0, :, :]
    inverse = 1.0 / density
    vel_x = conserved[..., 1, :, :] * inverse
    vel_y = conserved[..., 2, :, :] * inverse
    vel_z = conserved[..., 3, :, :] * inverse
    kinetic = 0.5 * (conserved[..., 1, :, :] * vel_x + conserved[..., 2, :, :] * vel_y + conserved[..., 3, :, :] * vel_z)
    pressure = (GAMMA - 1.0) * (conserved[..., 4, :, :] - kinetic)
    return jnp.stack([density, vel_x, vel_y, vel_z, pressure], axis=-3)

def euler_flux(primitive):
    density = primitive[..., 0, :, :]
    vel_x = primitive[..., 1, :, :]
    vel_y = primitive[..., 2, :, :]
    vel_z = primitive[..., 3, :, :]
    pressure = primitive[..., 4, :, :]
    mass_flux = density * vel_x
    energy = pressure / (GAMMA - 1.0) + 0.5 * density * (vel_x * vel_x + vel_y * vel_y + vel_z * vel_z)
    fluxes = jnp.stack([mass_flux, mass_flux * vel_x + pressure, mass_flux * vel_y, mass_flux * vel_z, vel_x * (energy + pressure)], axis=-3)
    conserved = jnp.stack([density, mass_flux, density * vel_y, density * vel_z, energy], axis=-3)
    speeds = jnp.abs(vel_x) + jnp.sqrt(GAMMA * pressure / density)
    return (fluxes, conserved, speeds)

def advance(block_volumes, lower_ghost, upper_ghost):
    extended = jnp.concatenate([lower_ghost, block_volumes, upper_ghost], axis=-2)
    primitive = primitives(extended)
    below_diff = primitive[..., 1:-1, :] - primitive[..., :-2, :]
    above_diff = primitive[..., 2:, :] - primitive[..., 1:-1, :]
    slopes = 0.5 * (jnp.sign(below_diff) + jnp.sign(above_diff)) * jnp.minimum(jnp.abs(below_diff), jnp.abs(above_diff))
    centre = primitive[..., 1:-1, :]
    left_state = (centre + 0.5 * slopes)[..., :-1, :]
    right_state = (centre - 0.5 * slopes)[..., 1:, :]
    left_flux, left_cons, left_speed = euler_flux(left_state)
    right_flux, right_cons, right_speed = euler_flux(right_state)
    largest = jnp.maximum(left_speed, right_speed)[..., None, :, :]
    interface = 0.5 * (left_flux + right_flux) - 0.5 * largest * (right_cons - left_cons)
    updated = block_volumes - COURANT * (interface[..., 1:, :] - interface[..., :-1, :])
    return (updated, interface[..., -1, :])

def fill_edges(block_volumes, lower_ghost, upper_ghost, lower_nbr, upper_nbr):
    first = block_volumes[:, :, :1, :]
    last = block_volumes[:, :, -1:, :]
    lower_ghost = jnp.where((lower_nbr < 0)[:, None, None, None], jnp.concatenate([first, first], axis=2), lower_ghost)
    upper_ghost = jnp.where((upper_nbr < 0)[:, None, None, None], jnp.concatenate([last, last], axis=2), upper_ghost)
    return (lower_ghost, upper_ghost)

def coarsen(interface):
    half_edge = SIDE_LENGTH // 2
    shaped = interface.reshape(interface.shape[:-1] + (half_edge, 2, half_edge, 2))
    return shaped.mean(axis=(-3, -1))

def spread(coarse, quadrant):
    half_edge = SIDE_LENGTH // 2
    tiled = jnp.tile(coarse, (1,) * (coarse.ndim - 2) + (2, 2))
    row_ids = jnp.arange(SIDE_LENGTH, dtype=jnp.int32) // half_edge
    inside = (row_ids[:, None] == (quadrant // 2)[..., None, None]) & (row_ids[None, :] == (quadrant % 2)[..., None, None])
    placed = tiled * inside.astype(tiled.dtype)[..., None, :, :]
    return placed.reshape(placed.shape[:-2] + (SIDE_LENGTH * SIDE_LENGTH,))

def reference(block_states, dest_dev, dest_slot, neighbours, coarse_map):
    group_size = N_DEV * DEVICE_PATCHES
    slot_group = jnp.arange(SLOTS_IN, dtype=jnp.int32) // (N_DEV * P_DEV)
    destination_position = jnp.where(dest_dev >= 0, (slot_group * N_DEV + dest_dev) * DEVICE_PATCHES + dest_slot, BLOCK_NUMBER).astype(jnp.int32)
    redistributed_blocks = jnp.zeros((BLOCK_NUMBER, STATE_VARIABLES, SIDE_LENGTH ** 3), block_states.dtype).at[destination_position].set(block_states, mode='drop')
    block_volumes = redistributed_blocks.reshape(BLOCK_NUMBER, STATE_VARIABLES, SIDE_LENGTH, SIDE_LENGTH * SIDE_LENGTH)
    slot_index = jnp.arange(BLOCK_NUMBER, dtype=jnp.int32)
    group_start = slot_index // group_size * group_size
    lower_src = jnp.where(neighbours[0] >= 0, group_start + neighbours[0], slot_index).astype(jnp.int32)
    upper_src = jnp.where(neighbours[1] >= 0, group_start + neighbours[1], slot_index).astype(jnp.int32)
    lower_ghost = block_volumes[:, :, SIDE_LENGTH - 2:, :][lower_src]
    upper_ghost = block_volumes[:, :, :2, :][upper_src]
    lower_ghost, upper_ghost = fill_edges(block_volumes, lower_ghost, upper_ghost, neighbours[0], neighbours[1])

    def one_group(operands):
        return advance(operands[0], operands[1], operands[2])
    advanced, interface = lax.map(one_group, (block_volumes.reshape(N_GRP, group_size, STATE_VARIABLES, SIDE_LENGTH, SIDE_LENGTH * SIDE_LENGTH), lower_ghost.reshape(N_GRP, group_size, STATE_VARIABLES, 2, SIDE_LENGTH * SIDE_LENGTH), upper_ghost.reshape(N_GRP, group_size, STATE_VARIABLES, 2, SIDE_LENGTH * SIDE_LENGTH)))
    advanced = advanced.reshape(BLOCK_NUMBER, STATE_VARIABLES, SIDE_LENGTH ** 3)
    interface = interface.reshape(BLOCK_NUMBER, STATE_VARIABLES, SIDE_LENGTH * SIDE_LENGTH)
    values = coarse_map.reshape(N_DEV, N_GRP, DEVICE_PATCHES).transpose(1, 0, 2).reshape(BLOCK_NUMBER)
    device = slot_index // DEVICE_PATCHES % N_DEV
    owner = (values // DEVICE_PATCHES * N_DEV + device).astype(jnp.int32)
    placed = spread(coarsen(interface), values % DEVICE_PATCHES)
    registers = jax.ops.segment_sum(placed, owner, num_segments=REGS)
    return (advanced, registers)
```

```python
import functools

import jax
import jax.numpy as jnp
from jax import lax
from jax.experimental import pallas as pl
from jax.experimental.pallas import tpu as pltpu
from jax.sharding import PartitionSpec as P

X_CHIPS = 4
FIELDS = 5
PATCHES = 4
SLOTS = 8
GAMMA = 1.4
COURANT = 0.2
MESH = pl.DeviceIdType.MESH
HIGHEST = lax.Precision.HIGHEST
HOPS = 3

FACE = 40
INNER = 120


def primitives(u):
    inverse = 1.0 / u[0]
    vx, vy, vz = u[1] * inverse, u[2] * inverse, u[3] * inverse
    kinetic = 0.5 * (u[1] * vx + u[2] * vy + u[3] * vz)
    return [u[0], vx, vy, vz, (GAMMA - 1.0) * (u[4] - kinetic)]


def half_slopes(below, centre, above):
    out = []
    for b, c, a in zip(below, centre, above):
        down, up = c - b, a - c
        slope = jnp.maximum(0.0, jnp.minimum(down, up)) + jnp.minimum(0.0, jnp.maximum(down, up))
        out.append(0.5 * slope)
    return out


def euler_flux(prim):
    r, vx, vy, vz, p = prim
    mass = r * vx
    energy = p * (1.0 / (GAMMA - 1.0)) + 0.5 * r * (vx * vx + vy * vy + vz * vz)
    flux = [mass, mass * vx + p, mass * vy, mass * vz, vx * (energy + p)]
    cons = [r, mass, r * vy, r * vz, energy]
    return flux, cons, jnp.abs(vx) + jnp.sqrt(GAMMA * p / r)


def interface(left_prim, left_half, right_prim, right_half):
    left = [c + s for c, s in zip(left_prim, left_half)]
    right = [c - s for c, s in zip(right_prim, right_half)]
    lf, lc, ls = euler_flux(left)
    rf, rc, rs = euler_flux(right)
    largest = 0.5 * jnp.maximum(ls, rs)
    return [0.5 * (a + b) - largest * (d - c) for a, b, c, d in zip(lf, rf, lc, rc)]


def iota(shape, dim):
    return lax.broadcasted_iota(jnp.int32, shape, dim)


def kernel(
    nz, nx, n_dev,
    blk, ddev, dslot, nbr, cmap,
    adv, reg,
    slot_face, slot_inner, face_send, face_recv, inner_send, inner_recv, near, outer, lower, upper, inner,
    xpool, zbuf, zrecv, adv_buf,
    face_ss, face_rs, inner_ss, inner_rs, ghost_ss, ghost_rs, x_ss, x_rs, z_ss, z_rs, out_sem,
):
    me = lax.axis_index("dev")
    grp = lax.axis_index("grp")
    mz, mx = grp // nx, grp % nx
    dev_at = lambda by: {"dev": lax.rem(me + by + n_dev, n_dev)}
    x_at = lambda by: {"grp": mz * nx + lax.rem(mx + by, nx)}
    z_at = lambda by: {"grp": lax.rem(mz + by, nz) * nx + mx}

    barrier = pltpu.get_barrier_semaphore()
    for by in (-1, -2, -3, 1):
        pl.semaphore_signal(barrier, inc=1, device_id=dev_at(by), device_id_type=MESH)
    for by in range(1, nx):
        pl.semaphore_signal(barrier, inc=1, device_id=x_at(by), device_id_type=MESH)
    for by in range(1, nz):
        pl.semaphore_signal(barrier, inc=1, device_id=z_at(by), device_id_type=MESH)

    for j in range(SLOTS):
        for f in range(FIELDS):
            for part, first in ((0, 0), (4, 28)):
                slot_face[j, pl.ds(f * 8 + part, 4), :] = blk[
                    pl.ds((f * 32 + first) * SLOTS + j, 4, stride=SLOTS), :]

    going = []
    for k in range(1, HOPS + 1):
        target = lax.rem(me + k, n_dev)
        slot = jnp.int32(0)
        for j in range(SLOTS):
            slot = jnp.where(ddev[me * SLOTS + j] == target, j, slot)
        going.append(slot)
    for k in range(HOPS):
        face_send[k] = slot_face[going[k]]

    pl.semaphore_wait(barrier, 4 + (nx - 1) + (nz - 1))

    face_copies = []
    for k in range(HOPS):
        copy = pltpu.make_async_remote_copy(
            src_ref=face_send.at[k], dst_ref=face_recv.at[k],
            send_sem=face_ss.at[k], recv_sem=face_rs.at[k], device_id=dev_at(k + 1), device_id_type=MESH)
        copy.start()
        face_copies.append(copy)

    own_slot = []
    for q in range(PATCHES):
        slot = jnp.int32(0)
        for j in range(SLOTS):
            i = me * SLOTS + j
            slot = jnp.where((ddev[i] == me) & (dslot[i] == q), j, slot)
        own_slot.append(slot)
    origin = [jnp.int32(0)] * PATCHES
    for k in range(1, HOPS + 1):
        source = lax.rem(me - k + n_dev, n_dev)
        landing = jnp.int32(-1)
        for j in range(SLOTS):
            i = source * SLOTS + j
            landing = jnp.where(ddev[i] == me, dslot[i], landing)
        for q in range(PATCHES):
            origin[q] = jnp.where(landing == q, k, origin[q])

    for j in range(SLOTS):
        for f in range(FIELDS):
            slot_inner[j, pl.ds(f * 24, 24), :] = blk[pl.ds((f * 32 + 4) * SLOTS + j, 24, stride=SLOTS), :]
    for k in range(HOPS):
        inner_send[k] = slot_inner[going[k]]

    lane32 = iota((8, 8 * nx), 1)
    row8 = iota((8, 8 * nx), 0)
    target = jnp.zeros((8, 8 * nx), jnp.int32)
    for i in range(nx):
        source = mz * nx + lax.rem(mx - i + nx, nx)
        for q in range(PATCHES):
            at = (lane32 >> 3 == i) & ((lane32 & 3) == q)
            target = jnp.where(at, cmap[0, source * PATCHES + q], target)
    same_half = (row8 >> 2) == ((lane32 >> 2) & 1)
    route = []
    for i in range(nz):
        code = (lax.rem(mz + i, nz) * nx + mx) * PATCHES
        hit = (target == code + (row8 & 3)) & same_half
        route.append(jnp.where(hit, 1.0, 0.0))
    route = jnp.concatenate(route, axis=0)

    for copy in face_copies:
        copy.wait_recv()
    for q in range(PATCHES):
        arrived = jnp.maximum(origin[q] - 1, 0)
        face = jnp.where(origin[q] > 0, face_recv[arrived], slot_face[own_slot[q]])
        near[PATCHES + q] = face
        outer[pl.ds(q, FACE, stride=PATCHES), :] = face

    ghost_copies = []
    for n, (by, first, to) in enumerate(((1, 1, 1), (-1, 0, 2 * PATCHES))):
        copy = pltpu.make_async_remote_copy(
            src_ref=near.at[pl.ds(PATCHES + first, 3)], dst_ref=near.at[pl.ds(to, 3)],
            send_sem=ghost_ss.at[n], recv_sem=ghost_rs.at[n], device_id=dev_at(by), device_id_type=MESH)
        copy.start()
        ghost_copies.append(copy)
    inner_copies = []
    for k in range(HOPS):
        copy = pltpu.make_async_remote_copy(
            src_ref=inner_send.at[k], dst_ref=inner_recv.at[k],
            send_sem=inner_ss.at[k], recv_sem=inner_rs.at[k], device_id=dev_at(k + 1), device_id_type=MESH)
        copy.start()
        inner_copies.append(copy)

    patch = iota((8, 128), 0) & 3
    lower_nbr = [nbr[0, me * PATCHES + q] for q in range(PATCHES)]
    upper_nbr = [nbr[1, me * PATCHES + q] for q in range(PATCHES)]
    lower_ids = jnp.zeros((8, 128), jnp.int32)
    upper_ids = jnp.zeros((8, 128), jnp.int32)
    for q in range(PATCHES):
        lower_ids = jnp.where(patch == q, lower_nbr[q], lower_ids)
        upper_ids = jnp.where(patch == q, upper_nbr[q], upper_ids)

    def neighbour(nb, q):
        place = jnp.where(nb < 0, PATCHES + q, nb - (me - 1) * PATCHES)
        return near[jnp.minimum(jnp.maximum(place, 0), 3 * PATCHES - 1)]

    for copy in ghost_copies:
        copy.wait_recv()
    for q in range(PATCHES):
        upper[pl.ds(q, FACE, stride=PATCHES), :] = neighbour(upper_nbr[q], q)

    own = lambda side, layer, f: outer[pl.ds(f * 32 + side * 16 + layer * 8, 8), :]
    last = [own(1, 1, f) for f in range(FIELDS)]
    ghosts_above = [
        [jnp.where(upper_ids < 0, last[f], upper[pl.ds(f * 32 + layer * 8, 8), :]) for f in range(FIELDS)]
        for layer in range(2)]
    p14 = primitives([own(1, 0, f) for f in range(FIELDS)])
    p15 = primitives(last)
    p16 = primitives(ghosts_above[0])
    p17 = primitives(ghosts_above[1])
    s15 = half_slopes(p14, p15, p16)
    s16 = half_slopes(p15, p16, p17)
    top_flux = interface(p15, s15, p16, s16)

    lane_in, lane_out = iota((128, 128), 0), iota((128, 128), 1)
    mean = jnp.where(
        (lane_in >> 5 == (lane_out >> 3) & 3) & ((lane_in & 15) >> 1 == (lane_out & 7)), 0.25, 0.0)
    coarse = jnp.dot(jnp.concatenate(top_flux, axis=0), mean, precision=HIGHEST, preferred_element_type=jnp.float32)
    lane8 = iota((8, 128), 1)
    packed = coarse[0:8]
    for f in range(1, 4):
        packed = jnp.where(lane8 >> 5 == f, coarse[f * 8:f * 8 + 8], packed)
    xpool[0:8, :] = packed
    xpool[8:16, :] = coarse[32:40]
    x_copies = []
    for i in range(1, nx):
        copy = pltpu.make_async_remote_copy(
            src_ref=xpool.at[pl.ds(0, 16)], dst_ref=xpool.at[pl.ds(i * 16, 16)],
            send_sem=x_ss.at[i - 1], recv_sem=x_rs.at[i - 1], device_id=x_at(i), device_id_type=MESH)
        copy.start()
        x_copies.append(copy)

    for q in range(PATCHES):
        lower[pl.ds(q, FACE, stride=PATCHES), :] = neighbour(lower_nbr[q], q)

    for copy in x_copies:
        copy.wait_recv()
    for v in range(2):
        pool = jnp.concatenate([xpool[i * 16 + v * 8:i * 16 + v * 8 + 8, :] for i in range(nx)], axis=0)
        routed = jnp.dot(route, pool, precision=HIGHEST, preferred_element_type=jnp.float32)
        for i in range(nz):
            zbuf[i * 16 + v * 8:i * 16 + v * 8 + 8, :] = routed[i * 8:i * 8 + 8]
    z_copies = []
    for i in range(1, nz):
        copy = pltpu.make_async_remote_copy(
            src_ref=zbuf.at[pl.ds(i * 16, 16)], dst_ref=zrecv.at[pl.ds((i - 1) * 16, 16)],
            send_sem=z_ss.at[i - 1], recv_sem=z_rs.at[i - 1], device_id=z_at(i), device_id_type=MESH)
        copy.start()
        z_copies.append(copy)

    for copy in inner_copies:
        copy.wait_recv()
    for q in range(PATCHES):
        arrived = jnp.maximum(origin[q] - 1, 0)
        for f in range(FIELDS):
            mine = slot_inner[own_slot[q], pl.ds(f * 24, 24), :]
            theirs = inner_recv[arrived, pl.ds(f * 24, 24), :]
            inner[pl.ds(f * 96 + q, 24, stride=PATCHES), :] = jnp.where(origin[q] > 0, theirs, mine)

    first = [own(0, 0, f) for f in range(FIELDS)]
    ghosts_below = [
        [jnp.where(lower_ids < 0, first[f], lower[pl.ds(f * 32 + 16 + layer * 8, 8), :]) for f in range(FIELDS)]
        for layer in range(2)]

    def layer(x):
        if x < 2:
            return [own(0, x, f) for f in range(FIELDS)]
        if x >= 14:
            return [own(1, x - 14, f) for f in range(FIELDS)]
        return [inner[pl.ds(f * 96 + (x - 2) * 8, 8), :] for f in range(FIELDS)]

    here, above = primitives(ghosts_below[1]), primitives(first)
    slope = half_slopes(primitives(ghosts_below[0]), here, above)
    below_flux = None
    for x in range(17):
        beyond = p17 if x == 16 else p16 if x == 15 else primitives(layer(x + 1))
        slope_above = half_slopes(here, above, beyond)
        flux = top_flux if x == 16 else interface(here, slope, above, slope_above)
        if x > 0:
            u = layer(x - 1)
            for f in range(FIELDS):
                adv_buf[pl.ds(f * 128 + (x - 1) * 8, 8), :] = u[f] - COURANT * (flux[f] - below_flux[f])
        here, above, slope, below_flux = above, beyond, slope_above, flux
    out = pltpu.make_async_copy(adv_buf, adv, out_sem)
    out.start()

    for copy in z_copies:
        copy.wait_recv()
    totals = []
    for v in range(2):
        total = zbuf[v * 8:v * 8 + 8, :]
        for i in range(nz - 1):
            total = total + zrecv[i * 16 + v * 8:i * 16 + v * 8 + 8, :]
        totals.append(total)
    parts = [jnp.where(lane8 >> 5 == f, totals[0], 0.0) for f in range(4)]
    parts.append(jnp.where(lane8 >> 5 == 0, totals[1], 0.0))
    place = jnp.where(
        (lane_in & 31) == ((lane_out >> 4) & 3) * 8 + (lane_out & 7), 1.0, 0.0)
    wide = jnp.dot(jnp.concatenate(parts, axis=0), place, precision=HIGHEST, preferred_element_type=jnp.float32)
    row = iota((8, 128), 0)
    inside = (row >> 2 == lane8 >> 6) & ((row & 1) == ((lane8 >> 3) & 1))
    for f in range(FIELDS):
        block = wide[f * 8:f * 8 + 8]
        for half in range(2):
            chosen = jnp.where(inside & ((row & 3) >> 1 == half), block, 0.0)
            reg[pl.ds(f * 2 + half, 1), :] = jnp.sum(chosen, axis=0, keepdims=True)

    for copy in face_copies + ghost_copies + inner_copies + x_copies + z_copies:
        copy.wait_send()
    out.wait()


def solution(mesh):
    n_grp, n_dev = mesh.shape["grp"], mesh.shape["dev"]
    nx = X_CHIPS
    nz = n_grp // nx

    def local(block_states, dest_dev, dest_slot, neighbours, coarse_map):
        blocks = block_states.reshape(SLOTS, FIELDS, 32, 128).transpose(1, 2, 0, 3).reshape(FIELDS * 32 * SLOTS, 128)
        vmem = pl.BlockSpec(memory_space=pltpu.VMEM)
        smem = pl.BlockSpec(memory_space=pltpu.SMEM)
        f32 = jnp.float32
        dma = lambda n: pltpu.SemaphoreType.DMA((n,))
        advanced, registers = pl.pallas_call(
            functools.partial(kernel, nz, nx, n_dev),
            out_shape=(jax.ShapeDtypeStruct((640, 128), f32), jax.ShapeDtypeStruct((10, 128), f32)),
            in_specs=[vmem, smem, smem, smem, smem],
            out_specs=(pl.BlockSpec(memory_space=pl.ANY), vmem),
            scratch_shapes=[
                pltpu.VMEM((SLOTS, FACE, 128), f32), pltpu.VMEM((SLOTS, INNER, 128), f32),
                pltpu.VMEM((HOPS, FACE, 128), f32), pltpu.VMEM((HOPS, FACE, 128), f32),
                pltpu.VMEM((HOPS, INNER, 128), f32), pltpu.VMEM((HOPS, INNER, 128), f32),
                pltpu.VMEM((3 * PATCHES, FACE, 128), f32), pltpu.VMEM((160, 128), f32),
                pltpu.VMEM((160, 128), f32), pltpu.VMEM((160, 128), f32),
                pltpu.VMEM((480, 128), f32),
                pltpu.VMEM((nx * 16, 128), f32), pltpu.VMEM((nz * 16, 128), f32), pltpu.VMEM(((nz - 1) * 16, 128), f32),
                pltpu.VMEM((640, 128), f32),
                dma(HOPS), dma(HOPS), dma(HOPS), dma(HOPS), dma(2), dma(2),
                dma(nx - 1), dma(nx - 1), dma(nz - 1), dma(nz - 1), pltpu.SemaphoreType.DMA,
            ],
            compiler_params=pltpu.CompilerParams(collective_id=0, has_side_effects=True),
        )(blocks, dest_dev, dest_slot, neighbours, coarse_map)
        advanced = advanced.reshape(FIELDS, 32, PATCHES, 128).transpose(2, 0, 1, 3).reshape(PATCHES, FIELDS, 4096)
        return advanced, registers.reshape(1, FIELDS, 256)

    in_specs = (P(("grp", "dev"), None, None), P("grp"), P("grp"), P(None, "grp"), P("dev", None))
    out_specs = (P(("grp", "dev"), None, None), P(("grp", "dev"), None, None))
    return jax.shard_map(local, mesh=mesh, in_specs=in_specs, out_specs=out_specs, check_vma=False)
```

```python
import functools

import jax
import jax.numpy as jnp
from jax import lax
from jax.experimental import pallas as pl
from jax.experimental.pallas import tpu as pltpu
from jax.sharding import PartitionSpec as P

X_CHIPS = 4
FIELDS = 5
PATCHES = 4
SLOTS = 8
GAMMA = 1.4
COURANT = 0.2
MESH = pl.DeviceIdType.MESH
HIGHEST = lax.Precision.HIGHEST
HOPS = 3

FACE = 40
INNER = 120


def primitives(u):
    inverse = 1.0 / u[0]
    vx, vy, vz = u[1] * inverse, u[2] * inverse, u[3] * inverse
    kinetic = 0.5 * (u[1] * vx + u[2] * vy + u[3] * vz)
    return [u[0], vx, vy, vz, (GAMMA - 1.0) * (u[4] - kinetic)]


def half_slopes(below, centre, above):
    out = []
    for b, c, a in zip(below, centre, above):
        down, up = c - b, a - c
        slope = jnp.maximum(0.0, jnp.minimum(down, up)) + jnp.minimum(0.0, jnp.maximum(down, up))
        out.append(0.5 * slope)
    return out


def euler_flux(prim):
    r, vx, vy, vz, p = prim
    mass = r * vx
    energy = p * (1.0 / (GAMMA - 1.0)) + 0.5 * r * (vx * vx + vy * vy + vz * vz)
    flux = [mass, mass * vx + p, mass * vy, mass * vz, vx * (energy + p)]
    cons = [r, mass, r * vy, r * vz, energy]
    return flux, cons, jnp.abs(vx) + jnp.sqrt(GAMMA * p / r)


def interface(left_prim, left_half, right_prim, right_half):
    left = [c + s for c, s in zip(left_prim, left_half)]
    right = [c - s for c, s in zip(right_prim, right_half)]
    lf, lc, ls = euler_flux(left)
    rf, rc, rs = euler_flux(right)
    largest = 0.5 * jnp.maximum(ls, rs)
    return [0.5 * (a + b) - largest * (d - c) for a, b, c, d in zip(lf, rf, lc, rc)]


def iota(shape, dim):
    return lax.broadcasted_iota(jnp.int32, shape, dim)


def kernel(
    nz, nx, n_dev,
    blk_hbm, ddev_hbm, dslot_hbm, nbr_hbm, cmap_hbm,
    adv, reg,
    blk, ddev, dslot, nbr, cmap,
    slot_face, slot_inner, face_send, face_recv, inner_send, inner_recv, near, outer, lower, upper, inner,
    xpool, zbuf, zrecv,
    face_ss, face_rs, inner_ss, inner_rs, ghost_ss, ghost_rs, x_ss, x_rs, z_ss, z_rs, in_sem,
):
    loads = []
    for n, (source, held) in enumerate(
        ((ddev_hbm, ddev), (blk_hbm, blk), (dslot_hbm, dslot), (nbr_hbm, nbr), (cmap_hbm, cmap))):
        copy = pltpu.make_async_copy(source, held, in_sem.at[n])
        copy.start()
        loads.append(copy)
    me = lax.axis_index("dev")
    grp = lax.axis_index("grp")
    mz, mx = grp // nx, grp % nx
    dev_at = lambda by: {"dev": lax.rem(me + by + n_dev, n_dev)}
    x_at = lambda by: {"grp": mz * nx + lax.rem(mx + by, nx)}
    z_at = lambda by: {"grp": lax.rem(mz + by, nz) * nx + mx}

    barrier = pltpu.get_barrier_semaphore()
    for by in (-1, -2, -3, 1):
        pl.semaphore_signal(barrier, inc=1, device_id=dev_at(by), device_id_type=MESH)
    for by in range(1, nx):
        pl.semaphore_signal(barrier, inc=1, device_id=x_at(by), device_id_type=MESH)
    for by in range(1, nz):
        pl.semaphore_signal(barrier, inc=1, device_id=z_at(by), device_id_type=MESH)

    for copy in loads:
        copy.wait()
    for j in range(SLOTS):
        for f in range(FIELDS):
            for part, first in ((0, 0), (4, 28)):
                slot_face[j, pl.ds(f * 8 + part, 4), :] = blk[
                    pl.ds((f * 32 + first) * SLOTS + j, 4, stride=SLOTS), :]

    going = []
    for k in range(1, HOPS + 1):
        target = lax.rem(me + k, n_dev)
        slot = jnp.int32(0)
        for j in range(SLOTS):
            slot = jnp.where(ddev[me * SLOTS + j] == target, j, slot)
        going.append(slot)
    for k in range(HOPS):
        face_send[k] = slot_face[going[k]]

    pl.semaphore_wait(barrier, 4 + (nx - 1) + (nz - 1))

    face_copies = []
    for k in range(HOPS):
        copy = pltpu.make_async_remote_copy(
            src_ref=face_send.at[k], dst_ref=face_recv.at[k],
            send_sem=face_ss.at[k], recv_sem=face_rs.at[k], device_id=dev_at(k + 1), device_id_type=MESH)
        copy.start()
        face_copies.append(copy)

    own_slot = []
    for q in range(PATCHES):
        slot = jnp.int32(0)
        for j in range(SLOTS):
            i = me * SLOTS + j
            slot = jnp.where((ddev[i] == me) & (dslot[i] == q), j, slot)
        own_slot.append(slot)
    origin = [jnp.int32(0)] * PATCHES
    for k in range(1, HOPS + 1):
        source = lax.rem(me - k + n_dev, n_dev)
        landing = jnp.int32(-1)
        for j in range(SLOTS):
            i = source * SLOTS + j
            landing = jnp.where(ddev[i] == me, dslot[i], landing)
        for q in range(PATCHES):
            origin[q] = jnp.where(landing == q, k, origin[q])

    for j in range(SLOTS):
        for f in range(FIELDS):
            slot_inner[j, pl.ds(f * 24, 24), :] = blk[pl.ds((f * 32 + 4) * SLOTS + j, 24, stride=SLOTS), :]
    for k in range(HOPS):
        inner_send[k] = slot_inner[going[k]]

    width = 8 * nx
    column = iota((8, 4 * width), 1)
    target = jnp.zeros((8, 4 * width), jnp.int32)
    for i in range(nx):
        source = mz * nx + lax.rem(mx - i + nx, nx)
        for q in range(PATCHES):
            at = (((column & (width - 1)) >> 3) == i) & ((column & 3) == q)
            target = jnp.where(at, cmap[0, source * PATCHES + q], target)
    row8 = iota((8, width), 0)
    same_half = (row8 >> 2) == ((iota((8, width), 1) >> 2) & 1)
    route = []
    for i in range(nz):
        code = (lax.rem(mz + i, nz) * nx + mx) * PATCHES
        route.append(jnp.where((target[:, :width] == code + (row8 & 3)) & same_half, 1.0, 0.0))
    route = jnp.concatenate(route, axis=0)
    wide_row, wide_column = iota((2 * nz, 4 * width), 0), iota((2 * nz, 4 * width), 1)
    place_z = mz + (wide_row >> 1)
    place_z = jnp.where(place_z >= nz, place_z - nz, place_z)
    code = (place_z * nx + mx) * PATCHES + sum((wide_column >= t * width).astype(jnp.int32) for t in range(1, 4))
    wide_target = jnp.broadcast_to(target[0:1], (2 * nz, 4 * width))
    wide_route = jnp.where((wide_target == code) & ((wide_row & 1) == ((wide_column >> 2) & 1)), 1.0, 0.0)

    for copy in face_copies:
        copy.wait_recv()
    for q in range(PATCHES):
        arrived = jnp.maximum(origin[q] - 1, 0)
        face = jnp.where(origin[q] > 0, face_recv[arrived], slot_face[own_slot[q]])
        near[PATCHES + q] = face
        outer[pl.ds(q, FACE, stride=PATCHES), :] = face

    ghost_copies = []
    for n, (by, first, to) in enumerate(((1, 1, 1), (-1, 0, 2 * PATCHES))):
        copy = pltpu.make_async_remote_copy(
            src_ref=near.at[pl.ds(PATCHES + first, 3)], dst_ref=near.at[pl.ds(to, 3)],
            send_sem=ghost_ss.at[n], recv_sem=ghost_rs.at[n], device_id=dev_at(by), device_id_type=MESH)
        copy.start()
        ghost_copies.append(copy)
    inner_copies = []
    for k in range(HOPS):
        copy = pltpu.make_async_remote_copy(
            src_ref=inner_send.at[k], dst_ref=inner_recv.at[k],
            send_sem=inner_ss.at[k], recv_sem=inner_rs.at[k], device_id=dev_at(k + 1), device_id_type=MESH)
        copy.start()
        inner_copies.append(copy)

    patch = iota((8, 128), 0) & 3
    lower_nbr = [nbr[0, me * PATCHES + q] for q in range(PATCHES)]
    upper_nbr = [nbr[1, me * PATCHES + q] for q in range(PATCHES)]
    lower_ids = jnp.zeros((8, 128), jnp.int32)
    upper_ids = jnp.zeros((8, 128), jnp.int32)
    for q in range(PATCHES):
        lower_ids = jnp.where(patch == q, lower_nbr[q], lower_ids)
        upper_ids = jnp.where(patch == q, upper_nbr[q], upper_ids)

    def neighbour(nb, q):
        place = jnp.where(nb < 0, PATCHES + q, nb - (me - 1) * PATCHES)
        return near[jnp.minimum(jnp.maximum(place, 0), 3 * PATCHES - 1)]

    for copy in ghost_copies:
        copy.wait_recv()
    for q in range(PATCHES):
        upper[pl.ds(q, FACE, stride=PATCHES), :] = neighbour(upper_nbr[q], q)

    own = lambda side, layer, f: outer[pl.ds(f * 32 + side * 16 + layer * 8, 8), :]
    last = [own(1, 1, f) for f in range(FIELDS)]
    ghosts_above = [
        [jnp.where(upper_ids < 0, last[f], upper[pl.ds(f * 32 + layer * 8, 8), :]) for f in range(FIELDS)]
        for layer in range(2)]
    p14 = primitives([own(1, 0, f) for f in range(FIELDS)])
    p15 = primitives(last)
    p16 = primitives(ghosts_above[0])
    p17 = primitives(ghosts_above[1])
    s15 = half_slopes(p14, p15, p16)
    s16 = half_slopes(p15, p16, p17)
    top_flux = interface(p15, s15, p16, s16)

    lane_in, lane_out = iota((128, 128), 0), iota((128, 128), 1)
    mean = jnp.where(
        (lane_in >> 5 == (lane_out >> 3) & 3) & ((lane_in & 15) >> 1 == (lane_out & 7)), 0.25, 0.0)
    coarse = jnp.dot(jnp.concatenate(top_flux, axis=0), mean, precision=HIGHEST, preferred_element_type=jnp.float32)
    lane8 = iota((8, 128), 1)
    packed = coarse[0:8]
    for f in range(1, 4):
        packed = jnp.where(lane8 >> 5 == f, coarse[f * 8:f * 8 + 8], packed)
    xpool[0:8, :] = packed
    xpool[8:16, :] = coarse[32:40]
    x_copies = []
    for i in range(1, nx):
        copy = pltpu.make_async_remote_copy(
            src_ref=xpool.at[pl.ds(0, 16)], dst_ref=xpool.at[pl.ds(i * 16, 16)],
            send_sem=x_ss.at[i - 1], recv_sem=x_rs.at[i - 1], device_id=x_at(i), device_id_type=MESH)
        copy.start()
        x_copies.append(copy)

    for q in range(PATCHES):
        lower[pl.ds(q, FACE, stride=PATCHES), :] = neighbour(lower_nbr[q], q)

    for copy in x_copies:
        copy.wait_recv()
    pool = jnp.concatenate([xpool[i * 16:i * 16 + 8, :] for i in range(nx)], axis=0)
    routed = jnp.dot(route, pool, precision=HIGHEST, preferred_element_type=jnp.float32)
    pool = jnp.concatenate([xpool[i * 16 + 8:i * 16 + 16, :] for i in range(nx)], axis=0)
    group = iota((width, 128), 1) >> 5
    pool = jnp.concatenate([jnp.where(group == t, pool, 0.0) for t in range(4)], axis=0)
    routed_fifth = jnp.dot(wide_route, pool, precision=HIGHEST, preferred_element_type=jnp.float32)
    for i in range(nz):
        zbuf[i, 0:8, :] = routed[i * 8:i * 8 + 8]
        zbuf[i, 8:10, :] = routed_fifth[i * 2:i * 2 + 2]
    z_copies = []
    for i in sorted(range(1, nz), key=lambda i: -min(i, nz - i)):
        copy = pltpu.make_async_remote_copy(
            src_ref=zbuf.at[i, pl.ds(0, 10)], dst_ref=zrecv.at[i - 1, pl.ds(0, 10)],
            send_sem=z_ss.at[i - 1], recv_sem=z_rs.at[i - 1], device_id=z_at(i), device_id_type=MESH)
        copy.start()
        z_copies.append(copy)

    for copy in inner_copies:
        copy.wait_recv()
    for q in range(PATCHES):
        arrived = jnp.maximum(origin[q] - 1, 0)
        for f in range(FIELDS):
            mine = slot_inner[own_slot[q], pl.ds(f * 24, 24), :]
            theirs = inner_recv[arrived, pl.ds(f * 24, 24), :]
            inner[pl.ds(f * 96 + q, 24, stride=PATCHES), :] = jnp.where(origin[q] > 0, theirs, mine)

    first = [own(0, 0, f) for f in range(FIELDS)]
    ghosts_below = [
        [jnp.where(lower_ids < 0, first[f], lower[pl.ds(f * 32 + 16 + layer * 8, 8), :]) for f in range(FIELDS)]
        for layer in range(2)]

    def layer(x):
        if x < 2:
            return [own(0, x, f) for f in range(FIELDS)]
        if x >= 14:
            return [own(1, x - 14, f) for f in range(FIELDS)]
        return [inner[pl.ds(f * 96 + (x - 2) * 8, 8), :] for f in range(FIELDS)]

    here, above = primitives(ghosts_below[1]), primitives(first)
    slope = half_slopes(primitives(ghosts_below[0]), here, above)
    below_flux = None
    for x in range(17):
        beyond = p17 if x == 16 else p16 if x == 15 else primitives(layer(x + 1))
        slope_above = half_slopes(here, above, beyond)
        flux = top_flux if x == 16 else interface(here, slope, above, slope_above)
        if x > 0:
            u = layer(x - 1)
            for f in range(FIELDS):
                adv[pl.ds(f * 128 + (x - 1) * 8, 8), :] = u[f] - COURANT * (flux[f] - below_flux[f])
        here, above, slope, below_flux = above, beyond, slope_above, flux

    for copy in z_copies:
        copy.wait_recv()
    total, fifth = zbuf[0, 0:8, :], zbuf[0, 8:10, :]
    for i in range(nz - 1):
        total = total + zrecv[i, 0:8, :]
        fifth = fifth + zrecv[i, 8:10, :]
    row = iota((8, 128), 0)
    fifth = jnp.where(row < 4, fifth[0:1], fifth[1:2])
    parts = [jnp.where(lane8 >> 5 == f, total, 0.0) for f in range(4)]
    parts.append(jnp.where(lane8 >> 5 == row & 3, fifth, 0.0))
    place = jnp.where(
        (lane_in & 31) == ((lane_out >> 4) & 3) * 8 + (lane_out & 7), 1.0, 0.0)
    wide = jnp.dot(jnp.concatenate(parts, axis=0), place, precision=HIGHEST, preferred_element_type=jnp.float32)
    inside = (row >> 2 == lane8 >> 6) & ((row & 1) == ((lane8 >> 3) & 1))
    for f in range(FIELDS):
        block = wide[f * 8:f * 8 + 8]
        for half in range(2):
            chosen = jnp.where(inside & ((row & 3) >> 1 == half), block, 0.0)
            reg[f, :, pl.ds(half * 128, 128)] = jnp.sum(chosen, axis=0, keepdims=True)

    for copy in face_copies + ghost_copies + inner_copies + x_copies + z_copies:
        copy.wait_send()


def solution(mesh):
    n_grp, n_dev = mesh.shape["grp"], mesh.shape["dev"]
    nx = X_CHIPS
    nz = n_grp // nx

    def local(block_states, dest_dev, dest_slot, neighbours, coarse_map):
        blocks = block_states.reshape(SLOTS, FIELDS, 32, 128).transpose(1, 2, 0, 3).reshape(FIELDS * 32 * SLOTS, 128)
        vmem = pl.BlockSpec(memory_space=pltpu.VMEM)
        hbm = pl.BlockSpec(memory_space=pltpu.HBM)
        f32 = jnp.float32
        dma = lambda n: pltpu.SemaphoreType.DMA((n,))
        advanced, registers = pl.pallas_call(
            functools.partial(kernel, nz, nx, n_dev),
            out_shape=(pltpu.VMEM((640, 128), f32), pltpu.VMEM((FIELDS, 1, 256), f32)),
            in_specs=[hbm] * 5,
            out_specs=(vmem, vmem),
            scratch_shapes=[
                pltpu.VMEM((1280, 128), f32), pltpu.SMEM(dest_dev.shape, jnp.int32), pltpu.SMEM(dest_slot.shape, jnp.int32),
                pltpu.SMEM(neighbours.shape, jnp.int32), pltpu.SMEM(coarse_map.shape, jnp.int32),
                pltpu.VMEM((SLOTS, FACE, 128), f32), pltpu.VMEM((SLOTS, INNER, 128), f32),
                pltpu.VMEM((HOPS, FACE, 128), f32), pltpu.VMEM((HOPS, FACE, 128), f32),
                pltpu.VMEM((HOPS, INNER, 128), f32), pltpu.VMEM((HOPS, INNER, 128), f32),
                pltpu.VMEM((3 * PATCHES, FACE, 128), f32), pltpu.VMEM((160, 128), f32),
                pltpu.VMEM((160, 128), f32), pltpu.VMEM((160, 128), f32),
                pltpu.VMEM((480, 128), f32),
                pltpu.VMEM((nx * 16, 128), f32), pltpu.VMEM((nz, 16, 128), f32), pltpu.VMEM((nz - 1, 16, 128), f32),
                dma(HOPS), dma(HOPS), dma(HOPS), dma(HOPS), dma(2), dma(2),
                dma(nx - 1), dma(nx - 1), dma(nz - 1), dma(nz - 1), dma(5),
            ],
            compiler_params=pltpu.CompilerParams(collective_id=0, has_side_effects=True, vmem_limit_bytes=24 * 1024 * 1024),
        )(*[pltpu.with_memory_space_constraint(a, pltpu.HBM) for a in (blocks, dest_dev, dest_slot, neighbours, coarse_map)])
        advanced = advanced.reshape(FIELDS, 32, PATCHES, 128).transpose(2, 0, 1, 3).reshape(PATCHES, FIELDS, 4096)
        return advanced, registers.transpose(1, 0, 2)

    in_specs = (P(("grp", "dev"), None, None), P("grp"), P("grp"), P(None, "grp"), P("dev", None))
    out_specs = (P(("grp", "dev"), None, None), P(("grp", "dev"), None, None))
    return jax.shard_map(local, mesh=mesh, in_specs=in_specs, out_specs=out_specs, check_vma=False)
```

```python
import functools

import jax
import jax.numpy as jnp
from jax import lax
from jax.experimental import pallas as pl
from jax.experimental.pallas import tpu as pltpu
from jax.sharding import PartitionSpec as P

X_CHIPS = 4
FIELDS = 5
PATCHES = 4
SLOTS = 8
GAMMA = 1.4
COURANT = 0.2
MESH = pl.DeviceIdType.MESH
HIGHEST = lax.Precision.HIGHEST
HOPS = 3

EDGE = 20
INNER = 120

AHEAD = (
    (4, 13, (("low", 3),)),
    (3, 10, (("low", 2), ("low", 3), ("high", 3))),
    (2, 6, (("low", 1), ("low", 2), ("low", 3), ("high", 2))),
    (1, 0, (("kept", 1), ("kept", 2), ("kept", 3), ("low", 1), ("low", 2), ("high", 1))),
    (-1, 14, (("kept", 0), ("kept", 1), ("kept", 2))),
)
SENT = 17
OWN = SENT
ENTRIES = SENT + PATCHES + 1
LOW_AT = ((None, 6, 10, 13), (None, 3, 7, 11), (None, OWN + PATCHES, 4, 8))
LOW_KEPT = (-1, OWN, 14)
HIGH_AT = (None, 5, 9, 12)


def primitives(u):
    inverse = 1.0 / u[0]
    vx, vy, vz = u[1] * inverse, u[2] * inverse, u[3] * inverse
    kinetic = 0.5 * (u[1] * vx + u[2] * vy + u[3] * vz)
    return [u[0], vx, vy, vz, (GAMMA - 1.0) * (u[4] - kinetic)]


def half_slopes(below, centre, above):
    out = []
    for b, c, a in zip(below, centre, above):
        down, up = c - b, a - c
        slope = jnp.maximum(0.0, jnp.minimum(down, up)) + jnp.minimum(0.0, jnp.maximum(down, up))
        out.append(0.5 * slope)
    return out


def euler_flux(prim):
    r, vx, vy, vz, p = prim
    mass = r * vx
    energy = p * (1.0 / (GAMMA - 1.0)) + 0.5 * r * (vx * vx + vy * vy + vz * vz)
    flux = [mass, mass * vx + p, mass * vy, mass * vz, vx * (energy + p)]
    cons = [r, mass, r * vy, r * vz, energy]
    return flux, cons, jnp.abs(vx) + jnp.sqrt(GAMMA * p / r)


def interface(left_prim, left_half, right_prim, right_half):
    left = [c + s for c, s in zip(left_prim, left_half)]
    right = [c - s for c, s in zip(right_prim, right_half)]
    lf, lc, ls = euler_flux(left)
    rf, rc, rs = euler_flux(right)
    largest = 0.5 * jnp.maximum(ls, rs)
    return [0.5 * (a + b) - largest * (d - c) for a, b, c, d in zip(lf, rf, lc, rc)]


def iota(shape, dim):
    return lax.broadcasted_iota(jnp.int32, shape, dim)


def kernel(
    nz, nx, n_dev,
    blk_hbm, ddev_hbm, dslot_hbm, nbr_hbm, cmap_hbm,
    adv, reg,
    blk, ddev, dslot, nbr, cmap, table,
    slot_low, slot_high, slot_inner, edge_send, edges, inner_send, inner_recv, near, low, high, lower, upper, inner,
    xpool, zbuf, zrecv,
    edge_ss, edge_rs, inner_ss, inner_rs, ghost_ss, ghost_rs, x_ss, x_rs, z_ss, z_rs, in_sem,
):
    loads = []
    top, bottom, middle = pl.ds(28 * SLOTS, 4 * SLOTS), pl.ds(0, 4 * SLOTS), pl.ds(4 * SLOTS, 24 * SLOTS)
    for n, (source, held) in enumerate((
        (ddev_hbm, ddev), (dslot_hbm, dslot),
        (blk_hbm.at[:, bottom], blk.at[:, bottom]), (blk_hbm.at[:, top], blk.at[:, top]),
        (nbr_hbm, nbr), (cmap_hbm, cmap), (blk_hbm.at[:, middle], blk.at[:, middle]))):
        copy = pltpu.make_async_copy(source, held, in_sem.at[n])
        copy.start()
        loads.append(copy)
    me = lax.axis_index("dev")
    grp = lax.axis_index("grp")
    mz, mx = grp // nx, grp % nx
    dev_at = lambda by: {"dev": lax.rem(me + by + n_dev, n_dev)}
    x_at = lambda by: {"grp": mz * nx + lax.rem(mx + by, nx)}
    z_at = lambda by: {"grp": lax.rem(mz + by, nz) * nx + mx}

    barrier = pltpu.get_barrier_semaphore()
    for by in (-1, 1, -2, -3, -4):
        pl.semaphore_signal(barrier, inc=1, device_id=dev_at(by), device_id_type=MESH)
    for by in range(1, nx):
        pl.semaphore_signal(barrier, inc=1, device_id=x_at(by), device_id_type=MESH)
    for by in range(1, nz):
        pl.semaphore_signal(barrier, inc=1, device_id=z_at(by), device_id_type=MESH)

    loads[0].wait()
    loads[1].wait()
    going = [None]
    for k in range(1, HOPS + 1):
        target = lax.rem(me + k, n_dev)
        slot = jnp.int32(0)
        for j in range(SLOTS):
            slot = jnp.where(ddev[me * SLOTS + j] == target, j, slot)
        going.append(slot)
    own_slot = []
    for q in range(PATCHES):
        slot = jnp.int32(0)
        for j in range(SLOTS):
            i = me * SLOTS + j
            slot = jnp.where((ddev[i] == me) & (dslot[i] == q), j, slot)
        own_slot.append(slot)

    loads[2].wait()
    loads[3].wait()
    for j in range(SLOTS):
        for f in range(FIELDS):
            slot_low[j, pl.ds(f * 4, 4), :] = blk[f, pl.ds(j, 4, stride=SLOTS), :]
            slot_high[j, pl.ds(f * 4, 4), :] = blk[f, pl.ds(28 * SLOTS + j, 4, stride=SLOTS), :]
    for _, first, entries in AHEAD:
        for n, (what, j) in enumerate(entries):
            if what == "high":
                edge_send[first + n] = slot_high[going[j]]
            else:
                edge_send[first + n] = slot_low[own_slot[j] if what == "kept" else going[j]]

    pl.semaphore_wait(barrier, 5 + (nx - 1) + (nz - 1))

    edge_copies = []
    for n, (by, first, entries) in enumerate(AHEAD):
        part = pl.ds(first, len(entries))
        copy = pltpu.make_async_remote_copy(
            src_ref=edge_send.at[part], dst_ref=edges.at[part],
            send_sem=edge_ss.at[n], recv_sem=edge_rs.at[n], device_id=dev_at(by), device_id_type=MESH)
        copy.start()
        edge_copies.append(copy)

    for q in range(PATCHES):
        edges[OWN + q] = slot_low[own_slot[q]]
    edges[OWN + PATCHES] = slot_low[going[1]]
    origin = [jnp.int32(0)] * PATCHES
    high_at = [jnp.int32(0)] * PATCHES
    low_at = []
    for beside in range(3):
        place = lax.rem(me + beside - 1 + n_dev, n_dev)
        at = [jnp.int32(min(max(LOW_KEPT[beside] + q, 0), ENTRIES - 1)) for q in range(PATCHES)]
        for k in range(1, HOPS + 1):
            source = lax.rem(place - k + n_dev, n_dev)
            landing = jnp.int32(-1)
            for j in range(SLOTS):
                i = source * SLOTS + j
                landing = jnp.where(ddev[i] == place, dslot[i], landing)
            for q in range(PATCHES):
                at[q] = jnp.where(landing == q, LOW_AT[beside][k], at[q])
                if beside == 1:
                    origin[q] = jnp.where(landing == q, k, origin[q])
                    high_at[q] = jnp.where(landing == q, HIGH_AT[k], high_at[q])
        for q in range(PATCHES):
            table[beside * PATCHES + q] = at[q]
        low_at.append(at)
    loads[4].wait()
    lower_nbr = [nbr[0, me * PATCHES + q] for q in range(PATCHES)]
    upper_nbr = [nbr[1, me * PATCHES + q] for q in range(PATCHES)]

    def place_of(nb, q):
        place = jnp.where(nb < 0, PATCHES + q, nb - (me - 1) * PATCHES)
        return jnp.minimum(jnp.maximum(place, 0), 3 * PATCHES - 1)

    above_at = [table[place_of(upper_nbr[q], q)] for q in range(PATCHES)]
    patch = iota((8, 128), 0) & 3
    lower_ids = jnp.zeros((8, 128), jnp.int32)
    upper_ids = jnp.zeros((8, 128), jnp.int32)
    for q in range(PATCHES):
        lower_ids = jnp.where(patch == q, lower_nbr[q], lower_ids)
        upper_ids = jnp.where(patch == q, upper_nbr[q], upper_ids)
    loads[5].wait()

    width = 8 * nx
    column = iota((8, 4 * width), 1)
    target = jnp.zeros((8, 4 * width), jnp.int32)
    for i in range(nx):
        source = mz * nx + lax.rem(mx - i + nx, nx)
        for q in range(PATCHES):
            at = (((column & (width - 1)) >> 3) == i) & ((column & 3) == q)
            target = jnp.where(at, cmap[0, source * PATCHES + q], target)
    row8 = iota((8, width), 0)
    same_half = (row8 >> 2) == ((iota((8, width), 1) >> 2) & 1)
    route = []
    for i in range(nz):
        code = (lax.rem(mz + i, nz) * nx + mx) * PATCHES
        route.append(jnp.where((target[:, :width] == code + (row8 & 3)) & same_half, 1.0, 0.0))
    route = jnp.concatenate(route, axis=0)
    wide_row, wide_column = iota((2 * nz, 4 * width), 0), iota((2 * nz, 4 * width), 1)
    place_z = mz + (wide_row >> 1)
    place_z = jnp.where(place_z >= nz, place_z - nz, place_z)
    code = (place_z * nx + mx) * PATCHES + sum((wide_column >= t * width).astype(jnp.int32) for t in range(1, 4))
    wide_target = jnp.broadcast_to(target[0:1], (2 * nz, 4 * width))
    wide_route = jnp.where((wide_target == code) & ((wide_row & 1) == ((wide_column >> 2) & 1)), 1.0, 0.0)

    for copy in edge_copies:
        copy.wait_recv()
    for q in range(PATCHES):
        edge = jnp.where(origin[q] > 0, edges[high_at[q]], slot_high[own_slot[q]])
        near[PATCHES + q] = edge
        high[pl.ds(q, EDGE, stride=PATCHES), :] = edge
        upper[pl.ds(q, EDGE, stride=PATCHES), :] = edges[above_at[q]]

    def outer(side, layer):
        return [side[pl.ds(f * 16 + layer * 8, 8), :] for f in range(FIELDS)]

    last = outer(high, 1)
    ghosts_above = [
        [jnp.where(upper_ids < 0, a, b) for a, b in zip(last, outer(upper, layer))] for layer in range(2)]
    p14 = primitives(outer(high, 0))
    p15 = primitives(last)
    p16 = primitives(ghosts_above[0])
    p17 = primitives(ghosts_above[1])
    s15 = half_slopes(p14, p15, p16)
    s16 = half_slopes(p15, p16, p17)
    top_flux = interface(p15, s15, p16, s16)

    lane_in, lane_out = iota((128, 128), 0), iota((128, 128), 1)
    mean = jnp.where(
        (lane_in >> 5 == (lane_out >> 3) & 3) & ((lane_in & 15) >> 1 == (lane_out & 7)), 0.25, 0.0)
    coarse = jnp.dot(jnp.concatenate(top_flux, axis=0), mean, precision=HIGHEST, preferred_element_type=jnp.float32)
    lane8 = iota((8, 128), 1)
    packed = coarse[0:8]
    for f in range(1, 4):
        packed = jnp.where(lane8 >> 5 == f, coarse[f * 8:f * 8 + 8], packed)
    xpool[0:8, :] = packed
    xpool[8:16, :] = coarse[32:40]
    x_copies = []
    for i in range(1, nx):
        copy = pltpu.make_async_remote_copy(
            src_ref=xpool.at[pl.ds(0, 16)], dst_ref=xpool.at[pl.ds(i * 16, 16)],
            send_sem=x_ss.at[i - 1], recv_sem=x_rs.at[i - 1], device_id=x_at(i), device_id_type=MESH)
        copy.start()
        x_copies.append(copy)

    ghost_copies = []
    for n, (by, first, to) in enumerate(((1, 1, 1), (-1, 0, 2 * PATCHES))):
        copy = pltpu.make_async_remote_copy(
            src_ref=near.at[pl.ds(PATCHES + first, 3)], dst_ref=near.at[pl.ds(to, 3)],
            send_sem=ghost_ss.at[n], recv_sem=ghost_rs.at[n], device_id=dev_at(by), device_id_type=MESH)
        copy.start()
        ghost_copies.append(copy)
    loads[6].wait()
    for j in range(SLOTS):
        for f in range(FIELDS):
            slot_inner[j, pl.ds(f * 24, 24), :] = blk[f, pl.ds(4 * SLOTS + j, 24, stride=SLOTS), :]
    inner_copies = []
    for k in range(HOPS):
        inner_send[k] = slot_inner[going[k + 1]]
        copy = pltpu.make_async_remote_copy(
            src_ref=inner_send.at[k], dst_ref=inner_recv.at[k],
            send_sem=inner_ss.at[k], recv_sem=inner_rs.at[k], device_id=dev_at(k + 1), device_id_type=MESH)
        copy.start()
        inner_copies.append(copy)

    for copy in x_copies:
        copy.wait_recv()
    pool = jnp.concatenate([xpool[i * 16:i * 16 + 8, :] for i in range(nx)], axis=0)
    routed = jnp.dot(route, pool, precision=HIGHEST, preferred_element_type=jnp.float32)
    pool = jnp.concatenate([xpool[i * 16 + 8:i * 16 + 16, :] for i in range(nx)], axis=0)
    group = iota((width, 128), 1) >> 5
    pool = jnp.concatenate([jnp.where(group == t, pool, 0.0) for t in range(4)], axis=0)
    routed_fifth = jnp.dot(wide_route, pool, precision=HIGHEST, preferred_element_type=jnp.float32)
    for i in range(nz):
        zbuf[i, 0:8, :] = routed[i * 8:i * 8 + 8]
        zbuf[i, 8:10, :] = routed_fifth[i * 2:i * 2 + 2]
    z_copies = []
    for i in sorted(range(1, nz), key=lambda i: -min(i, nz - i)):
        copy = pltpu.make_async_remote_copy(
            src_ref=zbuf.at[i, pl.ds(0, 10)], dst_ref=zrecv.at[i - 1, pl.ds(0, 10)],
            send_sem=z_ss.at[i - 1], recv_sem=z_rs.at[i - 1], device_id=z_at(i), device_id_type=MESH)
        copy.start()
        z_copies.append(copy)

    for copy in ghost_copies:
        copy.wait_recv()
    for q in range(PATCHES):
        low[pl.ds(q, EDGE, stride=PATCHES), :] = edges[low_at[1][q]]
        lower[pl.ds(q, EDGE, stride=PATCHES), :] = near[place_of(lower_nbr[q], q)]
    for copy in inner_copies:
        copy.wait_recv()
    for q in range(PATCHES):
        arrived = jnp.maximum(origin[q] - 1, 0)
        for f in range(FIELDS):
            mine = slot_inner[own_slot[q], pl.ds(f * 24, 24), :]
            theirs = inner_recv[arrived, pl.ds(f * 24, 24), :]
            inner[pl.ds(f * 96 + q, 24, stride=PATCHES), :] = jnp.where(origin[q] > 0, theirs, mine)

    first = outer(low, 0)
    ghosts_below = [
        [jnp.where(lower_ids < 0, a, b) for a, b in zip(first, outer(lower, layer))] for layer in range(2)]

    def layer(x):
        if x < 2:
            return outer(low, x)
        if x >= 14:
            return outer(high, x - 14)
        return [inner[pl.ds(f * 96 + (x - 2) * 8, 8), :] for f in range(FIELDS)]

    here, above = primitives(ghosts_below[1]), primitives(first)
    slope = half_slopes(primitives(ghosts_below[0]), here, above)
    below_flux = None
    for x in range(17):
        beyond = p17 if x == 16 else p16 if x == 15 else primitives(layer(x + 1))
        slope_above = half_slopes(here, above, beyond)
        flux = top_flux if x == 16 else interface(here, slope, above, slope_above)
        if x > 0:
            u = layer(x - 1)
            for f in range(FIELDS):
                adv[pl.ds(f * 128 + (x - 1) * 8, 8), :] = u[f] - COURANT * (flux[f] - below_flux[f])
        here, above, slope, below_flux = above, beyond, slope_above, flux

    for copy in z_copies:
        copy.wait_recv()
    total, fifth = zbuf[0, 0:8, :], zbuf[0, 8:10, :]
    for i in range(nz - 1):
        total = total + zrecv[i, 0:8, :]
        fifth = fifth + zrecv[i, 8:10, :]
    row = iota((8, 128), 0)
    fifth = jnp.where(row < 4, fifth[0:1], fifth[1:2])
    parts = [jnp.where(lane8 >> 5 == f, total, 0.0) for f in range(4)]
    parts.append(jnp.where(lane8 >> 5 == row & 3, fifth, 0.0))
    place = jnp.where(
        (lane_in & 31) == ((lane_out >> 4) & 3) * 8 + (lane_out & 7), 1.0, 0.0)
    wide = jnp.dot(jnp.concatenate(parts, axis=0), place, precision=HIGHEST, preferred_element_type=jnp.float32)
    inside = (row >> 2 == lane8 >> 6) & ((row & 1) == ((lane8 >> 3) & 1))
    for f in range(FIELDS):
        block = wide[f * 8:f * 8 + 8]
        for half in range(2):
            chosen = jnp.where(inside & ((row & 3) >> 1 == half), block, 0.0)
            reg[f, :, pl.ds(half * 128, 128)] = jnp.sum(chosen, axis=0, keepdims=True)

    for copy in edge_copies + ghost_copies + inner_copies + x_copies + z_copies:
        copy.wait_send()


def solution(mesh):
    n_grp, n_dev = mesh.shape["grp"], mesh.shape["dev"]
    nx = X_CHIPS
    nz = n_grp // nx

    def local(block_states, dest_dev, dest_slot, neighbours, coarse_map):
        blocks = block_states.reshape(SLOTS, FIELDS, 32, 128).transpose(1, 2, 0, 3).reshape(FIELDS, 32 * SLOTS, 128)
        vmem = pl.BlockSpec(memory_space=pltpu.VMEM)
        hbm = pl.BlockSpec(memory_space=pltpu.HBM)
        f32 = jnp.float32
        dma = lambda n: pltpu.SemaphoreType.DMA((n,))
        advanced, registers = pl.pallas_call(
            functools.partial(kernel, nz, nx, n_dev),
            out_shape=(pltpu.VMEM((640, 128), f32), pltpu.VMEM((FIELDS, 1, 256), f32)),
            in_specs=[hbm] * 5,
            out_specs=(vmem, vmem),
            scratch_shapes=[
                pltpu.VMEM((FIELDS, 32 * SLOTS, 128), f32), pltpu.SMEM(dest_dev.shape, jnp.int32), pltpu.SMEM(dest_slot.shape, jnp.int32),
                pltpu.SMEM(neighbours.shape, jnp.int32), pltpu.SMEM(coarse_map.shape, jnp.int32),
                pltpu.SMEM((3 * PATCHES,), jnp.int32),
                pltpu.VMEM((SLOTS, EDGE, 128), f32), pltpu.VMEM((SLOTS, EDGE, 128), f32),
                pltpu.VMEM((SLOTS, INNER, 128), f32),
                pltpu.VMEM((SENT, EDGE, 128), f32), pltpu.VMEM((ENTRIES, EDGE, 128), f32),
                pltpu.VMEM((HOPS, INNER, 128), f32), pltpu.VMEM((HOPS, INNER, 128), f32),
                pltpu.VMEM((3 * PATCHES, EDGE, 128), f32), pltpu.VMEM((80, 128), f32), pltpu.VMEM((80, 128), f32),
                pltpu.VMEM((80, 128), f32), pltpu.VMEM((80, 128), f32),
                pltpu.VMEM((480, 128), f32),
                pltpu.VMEM((nx * 16, 128), f32), pltpu.VMEM((nz, 16, 128), f32), pltpu.VMEM((max(nz - 1, 1), 16, 128), f32),
                dma(len(AHEAD)), dma(len(AHEAD)), dma(HOPS), dma(HOPS), dma(2), dma(2),
                dma(max(nx - 1, 1)), dma(max(nx - 1, 1)), dma(max(nz - 1, 1)), dma(max(nz - 1, 1)), dma(7),
            ],
            compiler_params=pltpu.CompilerParams(collective_id=0, has_side_effects=True, vmem_limit_bytes=24 * 1024 * 1024),
        )(*[pltpu.with_memory_space_constraint(a, pltpu.HBM) for a in (blocks, dest_dev, dest_slot, neighbours, coarse_map)])
        advanced = advanced.reshape(FIELDS, 32, PATCHES, 128).transpose(2, 0, 1, 3).reshape(PATCHES, FIELDS, 4096)
        return advanced, registers.transpose(1, 0, 2)

    in_specs = (P(("grp", "dev"), None, None), P("grp"), P("grp"), P(None, "grp"), P("dev", None))
    out_specs = (P(("grp", "dev"), None, None), P(("grp", "dev"), None, None))
    return jax.shard_map(local, mesh=mesh, in_specs=in_specs, out_specs=out_specs, check_vma=False)
```

```python
import functools

import jax
import jax.numpy as jnp
from jax import lax
from jax.experimental import pallas as pl
from jax.experimental.pallas import tpu as pltpu
from jax.sharding import PartitionSpec as P

X_CHIPS = 4
FIELDS = 5
PATCHES = 4
SLOTS = 8
GAMMA = 1.4
COURANT = 0.2
MESH = pl.DeviceIdType.MESH
HIGHEST = lax.Precision.HIGHEST
HOPS = 3

EDGE = 20
INNER = 120

AHEAD = (
    (4, 13, (("low", 3),)),
    (3, 10, (("low", 2), ("low", 3), ("high", 3))),
    (2, 6, (("low", 1), ("low", 2), ("low", 3), ("high", 2))),
    (1, 0, (("kept", 1), ("kept", 2), ("kept", 3), ("low", 1), ("low", 2), ("high", 1))),
    (-1, 14, (("kept", 0), ("kept", 1), ("kept", 2))),
)
SENT = 17
OWN = SENT
ENTRIES = SENT + PATCHES + 1
LOW_AT = ((None, 6, 10, 13), (None, 3, 7, 11), (None, OWN + PATCHES, 4, 8))
LOW_KEPT = (-1, OWN, 14)
HIGH_AT = (None, 5, 9, 12)


def primitives(u):
    inverse = 1.0 / u[0]
    vx, vy, vz = u[1] * inverse, u[2] * inverse, u[3] * inverse
    kinetic = 0.5 * (u[1] * vx + u[2] * vy + u[3] * vz)
    return [u[0], vx, vy, vz, (GAMMA - 1.0) * (u[4] - kinetic)]


def half_slopes(below, centre, above):
    out = []
    for b, c, a in zip(below, centre, above):
        down, up = c - b, a - c
        slope = jnp.maximum(0.0, jnp.minimum(down, up)) + jnp.minimum(0.0, jnp.maximum(down, up))
        out.append(0.5 * slope)
    return out


def euler_flux(prim):
    r, vx, vy, vz, p = prim
    mass = r * vx
    energy = p * (1.0 / (GAMMA - 1.0)) + 0.5 * r * (vx * vx + vy * vy + vz * vz)
    flux = [mass, mass * vx + p, mass * vy, mass * vz, vx * (energy + p)]
    cons = [r, mass, r * vy, r * vz, energy]
    return flux, cons, jnp.abs(vx) + jnp.sqrt(GAMMA * p / r)


def interface(left_prim, left_half, right_prim, right_half):
    left = [c + s for c, s in zip(left_prim, left_half)]
    right = [c - s for c, s in zip(right_prim, right_half)]
    lf, lc, ls = euler_flux(left)
    rf, rc, rs = euler_flux(right)
    largest = 0.5 * jnp.maximum(ls, rs)
    return [0.5 * (a + b) - largest * (d - c) for a, b, c, d in zip(lf, rf, lc, rc)]


def iota(shape, dim):
    return lax.broadcasted_iota(jnp.int32, shape, dim)


def kernel(
    nz, nx, n_dev,
    blk_hbm, ddev_hbm, dslot_hbm, nbr_hbm, cmap_hbm,
    adv, reg,
    blk, ddev, dslot, nbr, cmap, table,
    slot_low, slot_high, slot_inner, edge_send, edges, inner_send, inner_recv, near, low, high, lower, upper, inner,
    xpool, zbuf, zrecv,
    edge_ss, edge_rs, inner_ss, inner_rs, ghost_ss, ghost_rs, x_ss, x_rs, z_ss, z_rs, in_sem, ready,
):
    loads = []
    top, bottom, middle = pl.ds(28 * SLOTS, 4 * SLOTS), pl.ds(0, 4 * SLOTS), pl.ds(4 * SLOTS, 24 * SLOTS)
    for n, (source, held) in enumerate((
        (ddev_hbm, ddev), (dslot_hbm, dslot),
        (blk_hbm.at[:, bottom], blk.at[:, bottom]), (blk_hbm.at[:, top], blk.at[:, top]),
        (nbr_hbm, nbr), (cmap_hbm, cmap), (blk_hbm.at[:, middle], blk.at[:, middle]))):
        copy = pltpu.make_async_copy(source, held, in_sem.at[n])
        copy.start()
        loads.append(copy)
    me = lax.axis_index("dev")
    grp = lax.axis_index("grp")
    mz, mx = grp // nx, grp % nx
    dev_at = lambda by: {"dev": lax.rem(me + by + n_dev, n_dev)}
    x_at = lambda by: {"grp": mz * nx + lax.rem(mx + by, nx)}
    z_at = lambda by: {"grp": lax.rem(mz + by, nz) * nx + mx}

    barrier = pltpu.get_barrier_semaphore()
    for by in (-1, 1, -2, -3, -4):
        pl.semaphore_signal(barrier, inc=1, device_id=dev_at(by), device_id_type=MESH)
    for by in range(1, nx):
        pl.semaphore_signal(barrier, inc=1, device_id=x_at(by), device_id_type=MESH)
    for by in range(1, nz):
        @pl.when(mz + by < nz)
        def _():
            pl.semaphore_signal(barrier, inc=1, device_id=z_at(by), device_id_type=MESH)

    loads[0].wait()
    loads[1].wait()
    going = [None]
    for k in range(1, HOPS + 1):
        target = lax.rem(me + k, n_dev)
        slot = jnp.int32(0)
        for j in range(SLOTS):
            slot = jnp.where(ddev[me * SLOTS + j] == target, j, slot)
        going.append(slot)
    own_slot = []
    for q in range(PATCHES):
        slot = jnp.int32(0)
        for j in range(SLOTS):
            i = me * SLOTS + j
            slot = jnp.where((ddev[i] == me) & (dslot[i] == q), j, slot)
        own_slot.append(slot)

    loads[2].wait()
    loads[3].wait()
    for j in range(SLOTS):
        for f in range(FIELDS):
            slot_low[j, pl.ds(f * 4, 4), :] = blk[f, pl.ds(j, 4, stride=SLOTS), :]
            slot_high[j, pl.ds(f * 4, 4), :] = blk[f, pl.ds(28 * SLOTS + j, 4, stride=SLOTS), :]
    for _, first, entries in AHEAD:
        for n, (what, j) in enumerate(entries):
            if what == "high":
                edge_send[first + n] = slot_high[going[j]]
            else:
                edge_send[first + n] = slot_low[own_slot[j] if what == "kept" else going[j]]

    pl.semaphore_wait(barrier, 5 + (nx - 1) + mz)

    edge_copies = []
    for n, (by, first, entries) in enumerate(AHEAD):
        part = pl.ds(first, len(entries))
        copy = pltpu.make_async_remote_copy(
            src_ref=edge_send.at[part], dst_ref=edges.at[part],
            send_sem=edge_ss.at[n], recv_sem=edge_rs.at[n], device_id=dev_at(by), device_id_type=MESH)
        copy.start()
        edge_copies.append(copy)

    for by in range(1, nz):
        @pl.when(mz >= by)
        def _():
            pl.semaphore_signal(ready, inc=1, device_id=z_at(nz - by), device_id_type=MESH)

    for q in range(PATCHES):
        edges[OWN + q] = slot_low[own_slot[q]]
    edges[OWN + PATCHES] = slot_low[going[1]]
    origin = [jnp.int32(0)] * PATCHES
    high_at = [jnp.int32(0)] * PATCHES
    low_at = []
    for beside in range(3):
        place = lax.rem(me + beside - 1 + n_dev, n_dev)
        at = [jnp.int32(min(max(LOW_KEPT[beside] + q, 0), ENTRIES - 1)) for q in range(PATCHES)]
        for k in range(1, HOPS + 1):
            source = lax.rem(place - k + n_dev, n_dev)
            landing = jnp.int32(-1)
            for j in range(SLOTS):
                i = source * SLOTS + j
                landing = jnp.where(ddev[i] == place, dslot[i], landing)
            for q in range(PATCHES):
                at[q] = jnp.where(landing == q, LOW_AT[beside][k], at[q])
                if beside == 1:
                    origin[q] = jnp.where(landing == q, k, origin[q])
                    high_at[q] = jnp.where(landing == q, HIGH_AT[k], high_at[q])
        for q in range(PATCHES):
            table[beside * PATCHES + q] = at[q]
        low_at.append(at)
    loads[4].wait()
    lower_nbr = [nbr[0, me * PATCHES + q] for q in range(PATCHES)]
    upper_nbr = [nbr[1, me * PATCHES + q] for q in range(PATCHES)]

    def place_of(nb, q):
        place = jnp.where(nb < 0, PATCHES + q, nb - (me - 1) * PATCHES)
        return jnp.minimum(jnp.maximum(place, 0), 3 * PATCHES - 1)

    above_at = [table[place_of(upper_nbr[q], q)] for q in range(PATCHES)]
    patch = iota((8, 128), 0) & 3
    lower_ids = jnp.zeros((8, 128), jnp.int32)
    upper_ids = jnp.zeros((8, 128), jnp.int32)
    for q in range(PATCHES):
        lower_ids = jnp.where(patch == q, lower_nbr[q], lower_ids)
        upper_ids = jnp.where(patch == q, upper_nbr[q], upper_ids)
    loads[5].wait()

    width = 8 * nx
    column = iota((8, 4 * width), 1)
    target = jnp.zeros((8, 4 * width), jnp.int32)
    for i in range(nx):
        source = mz * nx + lax.rem(mx - i + nx, nx)
        for q in range(PATCHES):
            at = (((column & (width - 1)) >> 3) == i) & ((column & 3) == q)
            target = jnp.where(at, cmap[0, source * PATCHES + q], target)
    row8 = iota((8, width), 0)
    same_half = (row8 >> 2) == ((iota((8, width), 1) >> 2) & 1)
    route = []
    for i in range(nz):
        code = (lax.rem(mz + i, nz) * nx + mx) * PATCHES
        route.append(jnp.where((target[:, :width] == code + (row8 & 3)) & same_half, 1.0, 0.0))
    route = jnp.concatenate(route, axis=0)
    wide_row, wide_column = iota((2 * nz, 4 * width), 0), iota((2 * nz, 4 * width), 1)
    place_z = mz + (wide_row >> 1)
    place_z = jnp.where(place_z >= nz, place_z - nz, place_z)
    code = (place_z * nx + mx) * PATCHES + sum((wide_column >= t * width).astype(jnp.int32) for t in range(1, 4))
    wide_target = jnp.broadcast_to(target[0:1], (2 * nz, 4 * width))
    wide_route = jnp.where((wide_target == code) & ((wide_row & 1) == ((wide_column >> 2) & 1)), 1.0, 0.0)

    for copy in edge_copies:
        copy.wait_recv()
    for q in range(PATCHES):
        edge = jnp.where(origin[q] > 0, edges[high_at[q]], slot_high[own_slot[q]])
        near[PATCHES + q] = edge
        high[pl.ds(q, EDGE, stride=PATCHES), :] = edge
        upper[pl.ds(q, EDGE, stride=PATCHES), :] = edges[above_at[q]]

    def outer(side, layer):
        return [side[pl.ds(f * 16 + layer * 8, 8), :] for f in range(FIELDS)]

    last = outer(high, 1)
    ghosts_above = [
        [jnp.where(upper_ids < 0, a, b) for a, b in zip(last, outer(upper, layer))] for layer in range(2)]
    p14 = primitives(outer(high, 0))
    p15 = primitives(last)
    p16 = primitives(ghosts_above[0])
    p17 = primitives(ghosts_above[1])
    s15 = half_slopes(p14, p15, p16)
    s16 = half_slopes(p15, p16, p17)
    top_flux = interface(p15, s15, p16, s16)

    lane_in, lane_out = iota((128, 128), 0), iota((128, 128), 1)
    mean = jnp.where(
        (lane_in >> 5 == (lane_out >> 3) & 3) & ((lane_in & 15) >> 1 == (lane_out & 7)), 0.25, 0.0)
    coarse = jnp.dot(jnp.concatenate(top_flux, axis=0), mean, precision=HIGHEST, preferred_element_type=jnp.float32)
    lane8 = iota((8, 128), 1)
    packed = coarse[0:8]
    for f in range(1, 4):
        packed = jnp.where(lane8 >> 5 == f, coarse[f * 8:f * 8 + 8], packed)
    xpool[0:8, :] = packed
    xpool[8:16, :] = coarse[32:40]
    x_copies = []
    for i in range(1, nx):
        copy = pltpu.make_async_remote_copy(
            src_ref=xpool.at[pl.ds(0, 16)], dst_ref=xpool.at[pl.ds(i * 16, 16)],
            send_sem=x_ss.at[i - 1], recv_sem=x_rs.at[i - 1], device_id=x_at(i), device_id_type=MESH)
        copy.start()
        x_copies.append(copy)

    ghost_copies = []
    for n, (by, first, to) in enumerate(((1, 1, 1), (-1, 0, 2 * PATCHES))):
        copy = pltpu.make_async_remote_copy(
            src_ref=near.at[pl.ds(PATCHES + first, 3)], dst_ref=near.at[pl.ds(to, 3)],
            send_sem=ghost_ss.at[n], recv_sem=ghost_rs.at[n], device_id=dev_at(by), device_id_type=MESH)
        copy.start()
        ghost_copies.append(copy)
    loads[6].wait()
    for j in range(SLOTS):
        for f in range(FIELDS):
            slot_inner[j, pl.ds(f * 24, 24), :] = blk[f, pl.ds(4 * SLOTS + j, 24, stride=SLOTS), :]
    inner_copies = []
    for k in range(HOPS):
        inner_send[k] = slot_inner[going[k + 1]]
        copy = pltpu.make_async_remote_copy(
            src_ref=inner_send.at[k], dst_ref=inner_recv.at[k],
            send_sem=inner_ss.at[k], recv_sem=inner_rs.at[k], device_id=dev_at(k + 1), device_id_type=MESH)
        copy.start()
        inner_copies.append(copy)

    for copy in x_copies:
        copy.wait_recv()
    pool = jnp.concatenate([xpool[i * 16:i * 16 + 8, :] for i in range(nx)], axis=0)
    routed = jnp.dot(route, pool, precision=HIGHEST, preferred_element_type=jnp.float32)
    pool = jnp.concatenate([xpool[i * 16 + 8:i * 16 + 16, :] for i in range(nx)], axis=0)
    group = iota((width, 128), 1) >> 5
    pool = jnp.concatenate([jnp.where(group == t, pool, 0.0) for t in range(4)], axis=0)
    routed_fifth = jnp.dot(wide_route, pool, precision=HIGHEST, preferred_element_type=jnp.float32)
    for i in range(nz):
        zbuf[i, 0:8, :] = routed[i * 8:i * 8 + 8]
        zbuf[i, 8:10, :] = routed_fifth[i * 2:i * 2 + 2]
    z_copies = []
    for i in sorted(range(1, nz), key=lambda i: -min(i, nz - i)):
        copy = pltpu.make_async_remote_copy(
            src_ref=zbuf.at[i, pl.ds(0, 10)], dst_ref=zrecv.at[i - 1, pl.ds(0, 10)],
            send_sem=z_ss.at[i - 1], recv_sem=z_rs.at[i - 1], device_id=z_at(i), device_id_type=MESH)
        pl.when(mz + i >= nz)(copy.start)
        z_copies.append((i, copy))

    for copy in ghost_copies:
        copy.wait_recv()
    for q in range(PATCHES):
        low[pl.ds(q, EDGE, stride=PATCHES), :] = edges[low_at[1][q]]
        lower[pl.ds(q, EDGE, stride=PATCHES), :] = near[place_of(lower_nbr[q], q)]
    for copy in inner_copies:
        copy.wait_recv()
    for q in range(PATCHES):
        arrived = jnp.maximum(origin[q] - 1, 0)
        for f in range(FIELDS):
            mine = slot_inner[own_slot[q], pl.ds(f * 24, 24), :]
            theirs = inner_recv[arrived, pl.ds(f * 24, 24), :]
            inner[pl.ds(f * 96 + q, 24, stride=PATCHES), :] = jnp.where(origin[q] > 0, theirs, mine)

    first = outer(low, 0)
    ghosts_below = [
        [jnp.where(lower_ids < 0, a, b) for a, b in zip(first, outer(lower, layer))] for layer in range(2)]

    def layer(x):
        if x < 2:
            return outer(low, x)
        if x >= 14:
            return outer(high, x - 14)
        return [inner[pl.ds(f * 96 + (x - 2) * 8, 8), :] for f in range(FIELDS)]

    here, above = primitives(ghosts_below[1]), primitives(first)
    slope = half_slopes(primitives(ghosts_below[0]), here, above)
    below_flux = None
    for x in range(17):
        beyond = p17 if x == 16 else p16 if x == 15 else primitives(layer(x + 1))
        slope_above = half_slopes(here, above, beyond)
        flux = top_flux if x == 16 else interface(here, slope, above, slope_above)
        if x > 0:
            u = layer(x - 1)
            for f in range(FIELDS):
                adv[pl.ds(f * 128 + (x - 1) * 8, 8), :] = u[f] - COURANT * (flux[f] - below_flux[f])
        here, above, slope, below_flux = above, beyond, slope_above, flux

    @pl.when(mz < nz - 1)
    def _():
        pl.semaphore_wait(ready, nz - 1 - mz)
        for i, copy in z_copies:
            pl.when(mz + i < nz)(copy.start)
    z_copies = [copy for _, copy in z_copies]
    for copy in z_copies:
        copy.wait_recv()
    total, fifth = zbuf[0, 0:8, :], zbuf[0, 8:10, :]
    for i in range(nz - 1):
        total = total + zrecv[i, 0:8, :]
        fifth = fifth + zrecv[i, 8:10, :]
    row = iota((8, 128), 0)
    fifth = jnp.where(row < 4, fifth[0:1], fifth[1:2])
    parts = [jnp.where(lane8 >> 5 == f, total, 0.0) for f in range(4)]
    parts.append(jnp.where(lane8 >> 5 == row & 3, fifth, 0.0))
    place = jnp.where(
        (lane_in & 31) == ((lane_out >> 4) & 3) * 8 + (lane_out & 7), 1.0, 0.0)
    wide = jnp.dot(jnp.concatenate(parts, axis=0), place, precision=HIGHEST, preferred_element_type=jnp.float32)
    inside = (row >> 2 == lane8 >> 6) & ((row & 1) == ((lane8 >> 3) & 1))
    for f in range(FIELDS):
        block = wide[f * 8:f * 8 + 8]
        for half in range(2):
            chosen = jnp.where(inside & ((row & 3) >> 1 == half), block, 0.0)
            reg[f, :, pl.ds(half * 128, 128)] = jnp.sum(chosen, axis=0, keepdims=True)

    for copy in edge_copies + ghost_copies + inner_copies + x_copies + z_copies:
        copy.wait_send()


def solution(mesh):
    n_grp, n_dev = mesh.shape["grp"], mesh.shape["dev"]
    nx = X_CHIPS
    nz = n_grp // nx

    def local(block_states, dest_dev, dest_slot, neighbours, coarse_map):
        blocks = block_states.reshape(SLOTS, FIELDS, 32, 128).transpose(1, 2, 0, 3).reshape(FIELDS, 32 * SLOTS, 128)
        vmem = pl.BlockSpec(memory_space=pltpu.VMEM)
        hbm = pl.BlockSpec(memory_space=pltpu.HBM)
        f32 = jnp.float32
        dma = lambda n: pltpu.SemaphoreType.DMA((n,))
        advanced, registers = pl.pallas_call(
            functools.partial(kernel, nz, nx, n_dev),
            out_shape=(pltpu.VMEM((640, 128), f32), pltpu.VMEM((FIELDS, 1, 256), f32)),
            in_specs=[hbm] * 5,
            out_specs=(vmem, vmem),
            scratch_shapes=[
                pltpu.VMEM((FIELDS, 32 * SLOTS, 128), f32), pltpu.SMEM(dest_dev.shape, jnp.int32), pltpu.SMEM(dest_slot.shape, jnp.int32),
                pltpu.SMEM(neighbours.shape, jnp.int32), pltpu.SMEM(coarse_map.shape, jnp.int32),
                pltpu.SMEM((3 * PATCHES,), jnp.int32),
                pltpu.VMEM((SLOTS, EDGE, 128), f32), pltpu.VMEM((SLOTS, EDGE, 128), f32),
                pltpu.VMEM((SLOTS, INNER, 128), f32),
                pltpu.VMEM((SENT, EDGE, 128), f32), pltpu.VMEM((ENTRIES, EDGE, 128), f32),
                pltpu.VMEM((HOPS, INNER, 128), f32), pltpu.VMEM((HOPS, INNER, 128), f32),
                pltpu.VMEM((3 * PATCHES, EDGE, 128), f32), pltpu.VMEM((80, 128), f32), pltpu.VMEM((80, 128), f32),
                pltpu.VMEM((80, 128), f32), pltpu.VMEM((80, 128), f32),
                pltpu.VMEM((480, 128), f32),
                pltpu.VMEM((nx * 16, 128), f32), pltpu.VMEM((nz, 16, 128), f32), pltpu.VMEM((max(nz - 1, 1), 16, 128), f32),
                dma(len(AHEAD)), dma(len(AHEAD)), dma(HOPS), dma(HOPS), dma(2), dma(2),
                dma(max(nx - 1, 1)), dma(max(nx - 1, 1)), dma(max(nz - 1, 1)), dma(max(nz - 1, 1)), dma(7), pltpu.SemaphoreType.REGULAR,
            ],
            compiler_params=pltpu.CompilerParams(collective_id=0, has_side_effects=True, vmem_limit_bytes=24 * 1024 * 1024),
        )(*[pltpu.with_memory_space_constraint(a, pltpu.HBM) for a in (blocks, dest_dev, dest_slot, neighbours, coarse_map)])
        advanced = advanced.reshape(FIELDS, 32, PATCHES, 128).transpose(2, 0, 1, 3).reshape(PATCHES, FIELDS, 4096)
        return advanced, registers.transpose(1, 0, 2)

    in_specs = (P(("grp", "dev"), None, None), P("grp"), P("grp"), P(None, "grp"), P("dev", None))
    out_specs = (P(("grp", "dev"), None, None), P(("grp", "dev"), None, None))
    return jax.shard_map(local, mesh=mesh, in_specs=in_specs, out_specs=out_specs, check_vma=False)
```

```python
import functools

import jax
import jax.numpy as jnp
from jax import lax
from jax.experimental import pallas as pl
from jax.experimental.pallas import tpu as pltpu
from jax.sharding import PartitionSpec as P

X_CHIPS = 4
FIELDS = 5
PATCHES = 4
SLOTS = 8
GAMMA = 1.4
COURANT = 0.2
MESH = pl.DeviceIdType.MESH
HIGHEST = lax.Precision.HIGHEST
HOPS = 3

EDGE = 20
INNER = 120

AHEAD = (
    (4, 13, (("low", 3),)),
    (3, 10, (("low", 2), ("low", 3), ("high", 3))),
    (2, 6, (("low", 1), ("low", 2), ("low", 3), ("high", 2))),
    (1, 0, (("kept", 1), ("kept", 2), ("kept", 3), ("low", 1), ("low", 2), ("high", 1))),
    (-1, 14, (("kept", 0), ("kept", 1), ("kept", 2))),
)
SENT = 17
OWN = SENT
ENTRIES = SENT + PATCHES + 1
LOW_AT = ((None, 6, 10, 13), (None, 3, 7, 11), (None, OWN + PATCHES, 4, 8))
LOW_KEPT = (-1, OWN, 14)
HIGH_AT = (None, 5, 9, 12)


def primitives(u):
    inverse = 1.0 / u[0]
    vx, vy, vz = u[1] * inverse, u[2] * inverse, u[3] * inverse
    kinetic = 0.5 * (u[1] * vx + u[2] * vy + u[3] * vz)
    return [u[0], vx, vy, vz, (GAMMA - 1.0) * (u[4] - kinetic)]


def half_slopes(below, centre, above):
    out = []
    for b, c, a in zip(below, centre, above):
        down, up = c - b, a - c
        slope = jnp.maximum(0.0, jnp.minimum(down, up)) + jnp.minimum(0.0, jnp.maximum(down, up))
        out.append(0.5 * slope)
    return out


def euler_flux(prim):
    r, vx, vy, vz, p = prim
    mass = r * vx
    energy = p * (1.0 / (GAMMA - 1.0)) + 0.5 * r * (vx * vx + vy * vy + vz * vz)
    flux = [mass, mass * vx + p, mass * vy, mass * vz, vx * (energy + p)]
    cons = [r, mass, r * vy, r * vz, energy]
    return flux, cons, jnp.abs(vx) + jnp.sqrt(GAMMA * p / r)


def interface(left_prim, left_half, right_prim, right_half):
    left = [c + s for c, s in zip(left_prim, left_half)]
    right = [c - s for c, s in zip(right_prim, right_half)]
    lf, lc, ls = euler_flux(left)
    rf, rc, rs = euler_flux(right)
    largest = 0.5 * jnp.maximum(ls, rs)
    return [0.5 * (a + b) - largest * (d - c) for a, b, c, d in zip(lf, rf, lc, rc)]


def iota(shape, dim):
    return lax.broadcasted_iota(jnp.int32, shape, dim)


def kernel(
    nz, nx, n_dev,
    blk_hbm, ddev_hbm, dslot_hbm, nbr_hbm, cmap_hbm,
    adv, sums,
    blk, ddev, dslot, nbr, cmap, table,
    slot_low, slot_high, slot_inner, edge_send, edges, inner_send, inner_recv, near, low, high, lower, upper, inner,
    xpool, zbuf, zrecv,
    edge_ss, edge_rs, inner_ss, inner_rs, ghost_ss, ghost_rs, x_ss, x_rs, z_ss, z_rs, in_sem, ready,
):
    me = lax.axis_index("dev")
    grp = lax.axis_index("grp")
    mz, mx = grp >> (nx.bit_length() - 1), grp & (nx - 1)
    dev_of = lambda place: place & (n_dev - 1)
    z_of = lambda by: jnp.where(mz + by >= nz, mz + (by - nz), mz + by)
    dev_at = lambda by: (grp, dev_of(me + by))
    x_at = lambda by: ((grp - mx) + ((mx + by) & (nx - 1)), me)
    z_at = lambda by: (z_of(by) * nx + mx, me)

    barrier = pltpu.get_barrier_semaphore()
    for by in (-1, 1, -2, -3, -4):
        pl.semaphore_signal(barrier, inc=1, device_id=dev_at(by), device_id_type=MESH)
    for by in range(1, nx):
        pl.semaphore_signal(barrier, inc=1, device_id=x_at(by), device_id_type=MESH)
    loads = []
    top, bottom, middle = pl.ds(28 * SLOTS, 4 * SLOTS), pl.ds(0, 4 * SLOTS), pl.ds(4 * SLOTS, 24 * SLOTS)
    for n, (source, held) in enumerate((
        (ddev_hbm, ddev), (dslot_hbm, dslot),
        (blk_hbm.at[:, bottom], blk.at[:, bottom]), (blk_hbm.at[:, top], blk.at[:, top]),
        (nbr_hbm, nbr), (cmap_hbm, cmap), (blk_hbm.at[:, middle], blk.at[:, middle]))):
        copy = pltpu.make_async_copy(source, held, in_sem.at[n])
        copy.start()
        loads.append(copy)
    for by in range(1, nz):
        @pl.when(mz + by < nz)
        def _():
            pl.semaphore_signal(barrier, inc=1, device_id=z_at(by), device_id_type=MESH)

    loads[0].wait()
    loads[1].wait()
    going = [None]
    for k in range(1, HOPS + 1):
        target = dev_of(me + k)
        slot = jnp.int32(0)
        for j in range(SLOTS):
            slot = jnp.where(ddev[me * SLOTS + j] == target, j, slot)
        going.append(slot)
    own_slot = []
    for q in range(PATCHES):
        slot = jnp.int32(0)
        for j in range(SLOTS):
            i = me * SLOTS + j
            slot = jnp.where((ddev[i] == me) & (dslot[i] == q), j, slot)
        own_slot.append(slot)

    loads[2].wait()
    loads[3].wait()
    for j in range(SLOTS):
        for f in range(FIELDS):
            slot_low[j, pl.ds(f * 4, 4), :] = blk[f, pl.ds(j, 4, stride=SLOTS), :]
            slot_high[j, pl.ds(f * 4, 4), :] = blk[f, pl.ds(28 * SLOTS + j, 4, stride=SLOTS), :]
    for _, first, entries in AHEAD:
        for n, (what, j) in enumerate(entries):
            if what == "high":
                edge_send[first + n] = slot_high[going[j]]
            else:
                edge_send[first + n] = slot_low[own_slot[j] if what == "kept" else going[j]]

    pl.semaphore_wait(barrier, 5 + (nx - 1) + mz)

    edge_copies = []
    for n, (by, first, entries) in enumerate(AHEAD):
        part = pl.ds(first, len(entries))
        copy = pltpu.make_async_remote_copy(
            src_ref=edge_send.at[part], dst_ref=edges.at[part],
            send_sem=edge_ss.at[n], recv_sem=edge_rs.at[n], device_id=dev_at(by), device_id_type=MESH)
        copy.start()
        edge_copies.append(copy)

    for by in range(1, nz):
        @pl.when(mz >= by)
        def _():
            pl.semaphore_signal(ready, inc=1, device_id=z_at(nz - by), device_id_type=MESH)

    for q in range(PATCHES):
        edges[OWN + q] = slot_low[own_slot[q]]
    edges[OWN + PATCHES] = slot_low[going[1]]
    origin = [jnp.int32(0)] * PATCHES
    high_at = [jnp.int32(0)] * PATCHES
    low_at = []
    for beside in range(3):
        place = dev_of(me + beside - 1)
        at = [jnp.int32(min(max(LOW_KEPT[beside] + q, 0), ENTRIES - 1)) for q in range(PATCHES)]
        for k in range(1, HOPS + 1):
            source = dev_of(place - k)
            landing = jnp.int32(-1)
            for j in range(SLOTS):
                i = source * SLOTS + j
                landing = jnp.where(ddev[i] == place, dslot[i], landing)
            for q in range(PATCHES):
                at[q] = jnp.where(landing == q, LOW_AT[beside][k], at[q])
                if beside == 1:
                    origin[q] = jnp.where(landing == q, k, origin[q])
                    high_at[q] = jnp.where(landing == q, HIGH_AT[k], high_at[q])
        for q in range(PATCHES):
            table[beside * PATCHES + q] = at[q]
        low_at.append(at)
    loads[4].wait()
    lower_nbr = [nbr[0, me * PATCHES + q] for q in range(PATCHES)]
    upper_nbr = [nbr[1, me * PATCHES + q] for q in range(PATCHES)]

    def place_of(nb, q):
        place = jnp.where(nb < 0, PATCHES + q, nb - (me - 1) * PATCHES)
        return jnp.minimum(jnp.maximum(place, 0), 3 * PATCHES - 1)

    above_at = [table[place_of(upper_nbr[q], q)] for q in range(PATCHES)]
    patch = iota((8, 128), 0) & 3
    lower_ids = jnp.zeros((8, 128), jnp.int32)
    upper_ids = jnp.zeros((8, 128), jnp.int32)
    for q in range(PATCHES):
        lower_ids = jnp.where(patch == q, lower_nbr[q], lower_ids)
        upper_ids = jnp.where(patch == q, upper_nbr[q], upper_ids)
    loads[5].wait()

    width = 8 * nx
    column = iota((8, 4 * width), 1)
    target = jnp.zeros((8, 4 * width), jnp.int32)
    for i in range(nx):
        source = (grp - mx) + ((mx - i) & (nx - 1))
        for q in range(PATCHES):
            at = (((column & (width - 1)) >> 3) == i) & ((column & 3) == q)
            target = jnp.where(at, cmap[0, source * PATCHES + q], target)
    row8 = iota((8, width), 0)
    same_half = (row8 >> 2) == ((iota((8, width), 1) >> 2) & 1)
    route = []
    for i in range(nz):
        code = (z_of(i) * nx + mx) * PATCHES
        route.append(jnp.where((target[:, :width] == code + (row8 & 3)) & same_half, 1.0, 0.0))
    route = jnp.concatenate(route, axis=0)
    wide_row, wide_column = iota((2 * nz, 4 * width), 0), iota((2 * nz, 4 * width), 1)
    place_z = mz + (wide_row >> 1)
    place_z = jnp.where(place_z >= nz, place_z - nz, place_z)
    code = (place_z * nx + mx) * PATCHES + sum((wide_column >= t * width).astype(jnp.int32) for t in range(1, 4))
    wide_target = jnp.broadcast_to(target[0:1], (2 * nz, 4 * width))
    wide_route = jnp.where((wide_target == code) & ((wide_row & 1) == ((wide_column >> 2) & 1)), 1.0, 0.0)

    for copy in edge_copies:
        copy.wait_recv()
    for q in range(PATCHES):
        edge = jnp.where(origin[q] > 0, edges[high_at[q]], slot_high[own_slot[q]])
        near[PATCHES + q] = edge
        high[pl.ds(q, EDGE, stride=PATCHES), :] = edge
        upper[pl.ds(q, EDGE, stride=PATCHES), :] = edges[above_at[q]]

    def outer(side, layer):
        return [side[pl.ds(f * 16 + layer * 8, 8), :] for f in range(FIELDS)]

    last = outer(high, 1)
    ghosts_above = [
        [jnp.where(upper_ids < 0, a, b) for a, b in zip(last, outer(upper, layer))] for layer in range(2)]
    p14 = primitives(outer(high, 0))
    p15 = primitives(last)
    p16 = primitives(ghosts_above[0])
    p17 = primitives(ghosts_above[1])
    s15 = half_slopes(p14, p15, p16)
    s16 = half_slopes(p15, p16, p17)
    top_flux = interface(p15, s15, p16, s16)

    lane_in, lane_out = iota((128, 128), 0), iota((128, 128), 1)
    mean = jnp.where(
        (lane_in >> 5 == (lane_out >> 3) & 3) & ((lane_in & 15) >> 1 == (lane_out & 7)), 0.25, 0.0)
    coarse = jnp.dot(jnp.concatenate(top_flux, axis=0), mean, precision=HIGHEST, preferred_element_type=jnp.float32)
    lane8 = iota((8, 128), 1)
    packed = coarse[0:8]
    for f in range(1, 4):
        packed = jnp.where(lane8 >> 5 == f, coarse[f * 8:f * 8 + 8], packed)
    xpool[0:8, :] = packed
    xpool[8:16, :] = coarse[32:40]
    x_copies = []
    for i in range(1, nx):
        copy = pltpu.make_async_remote_copy(
            src_ref=xpool.at[pl.ds(0, 16)], dst_ref=xpool.at[pl.ds(i * 16, 16)],
            send_sem=x_ss.at[i - 1], recv_sem=x_rs.at[i - 1], device_id=x_at(i), device_id_type=MESH)
        copy.start()
        x_copies.append(copy)

    for copy in x_copies:
        copy.wait_recv()
    pool = jnp.concatenate([xpool[i * 16:i * 16 + 8, :] for i in range(nx)], axis=0)
    routed = jnp.dot(route, pool, precision=HIGHEST, preferred_element_type=jnp.float32)
    pool = jnp.concatenate([xpool[i * 16 + 8:i * 16 + 16, :] for i in range(nx)], axis=0)
    group = iota((width, 128), 1) >> 5
    pool = jnp.concatenate([jnp.where(group == t, pool, 0.0) for t in range(4)], axis=0)
    routed_fifth = jnp.dot(wide_route, pool, precision=HIGHEST, preferred_element_type=jnp.float32)
    for i in range(nz):
        zbuf[i, 0:8, :] = routed[i * 8:i * 8 + 8]
        zbuf[i, 8:10, :] = routed_fifth[i * 2:i * 2 + 2]
    z_copies = []
    for i in range(1, nz):
        copy = pltpu.make_async_remote_copy(
            src_ref=zbuf.at[i, pl.ds(0, 10)], dst_ref=zrecv.at[i - 1, pl.ds(0, 10)],
            send_sem=z_ss.at[i - 1], recv_sem=z_rs.at[i - 1], device_id=z_at(i), device_id_type=MESH)
        pl.when(mz + i >= nz)(copy.start)
        z_copies.append((i, copy))

    ghost_copies = []
    for n, (by, first, to) in enumerate(((1, 1, 1), (-1, 0, 2 * PATCHES))):
        copy = pltpu.make_async_remote_copy(
            src_ref=near.at[pl.ds(PATCHES + first, 3)], dst_ref=near.at[pl.ds(to, 3)],
            send_sem=ghost_ss.at[n], recv_sem=ghost_rs.at[n], device_id=dev_at(by), device_id_type=MESH)
        copy.start()
        ghost_copies.append(copy)
    loads[6].wait()
    for j in range(SLOTS):
        for f in range(FIELDS):
            slot_inner[j, pl.ds(f * 24, 24), :] = blk[f, pl.ds(4 * SLOTS + j, 24, stride=SLOTS), :]
    inner_copies = []
    for k in range(HOPS):
        inner_send[k] = slot_inner[going[k + 1]]
        copy = pltpu.make_async_remote_copy(
            src_ref=inner_send.at[k], dst_ref=inner_recv.at[k],
            send_sem=inner_ss.at[k], recv_sem=inner_rs.at[k], device_id=dev_at(k + 1), device_id_type=MESH)
        copy.start()
        inner_copies.append(copy)

    for copy in ghost_copies:
        copy.wait_recv()
    for q in range(PATCHES):
        low[pl.ds(q, EDGE, stride=PATCHES), :] = edges[low_at[1][q]]
        lower[pl.ds(q, EDGE, stride=PATCHES), :] = near[place_of(lower_nbr[q], q)]
    for copy in inner_copies:
        copy.wait_recv()
    for q in range(PATCHES):
        arrived = jnp.maximum(origin[q] - 1, 0)
        for f in range(FIELDS):
            mine = slot_inner[own_slot[q], pl.ds(f * 24, 24), :]
            theirs = inner_recv[arrived, pl.ds(f * 24, 24), :]
            inner[pl.ds(f * 96 + q, 24, stride=PATCHES), :] = jnp.where(origin[q] > 0, theirs, mine)

    first = outer(low, 0)
    ghosts_below = [
        [jnp.where(lower_ids < 0, a, b) for a, b in zip(first, outer(lower, layer))] for layer in range(2)]

    def layer(x):
        if x < 2:
            return outer(low, x)
        if x >= 14:
            return outer(high, x - 14)
        return [inner[pl.ds(f * 96 + (x - 2) * 8, 8), :] for f in range(FIELDS)]

    here, above = primitives(ghosts_below[1]), primitives(first)
    slope = half_slopes(primitives(ghosts_below[0]), here, above)
    below_flux = None
    for x in range(17):
        beyond = p17 if x == 16 else p16 if x == 15 else primitives(layer(x + 1))
        slope_above = half_slopes(here, above, beyond)
        flux = top_flux if x == 16 else interface(here, slope, above, slope_above)
        if x > 0:
            u = layer(x - 1)
            for f in range(FIELDS):
                adv[pl.ds(f * 128 + (x - 1) * 8, 8), :] = u[f] - COURANT * (flux[f] - below_flux[f])
        here, above, slope, below_flux = above, beyond, slope_above, flux

    @pl.when(mz < nz - 1)
    def _():
        pl.semaphore_wait(ready, nz - 1 - mz)
        for i, copy in z_copies:
            pl.when(mz + i < nz)(copy.start)
    z_copies = [copy for _, copy in z_copies]
    for copy in z_copies:
        copy.wait_recv()
    total, fifth = zbuf[0, 0:8, :], zbuf[0, 8:10, :]
    for i in range(nz - 1):
        total = total + zrecv[i, 0:8, :]
        fifth = fifth + zrecv[i, 8:10, :]
    sums[0:8, :] = total
    sums[8:10, :] = fifth

    for copy in edge_copies + ghost_copies + inner_copies + x_copies + z_copies:
        copy.wait_send()


def finish(adv, sums, adv_out, reg_out, reg_buf, adv_sem, reg_sem):
    adv_copy = pltpu.make_async_copy(adv, adv_out, adv_sem)
    adv_copy.start()
    lane_in, lane_out = iota((128, 128), 0), iota((128, 128), 1)
    lane8 = iota((8, 128), 1)
    total, fifth = sums[0:8, :], sums[8:10, :]
    row = iota((8, 128), 0)
    fifth = jnp.where(row < 4, fifth[0:1], fifth[1:2])
    parts = [jnp.where(lane8 >> 5 == f, total, 0.0) for f in range(4)]
    parts.append(jnp.where(lane8 >> 5 == row & 3, fifth, 0.0))
    place = jnp.where(
        (lane_in & 31) == ((lane_out >> 4) & 3) * 8 + (lane_out & 7), 1.0, 0.0)
    wide = jnp.dot(jnp.concatenate(parts, axis=0), place, precision=HIGHEST, preferred_element_type=jnp.float32)
    inside = (row >> 2 == lane8 >> 6) & ((row & 1) == ((lane8 >> 3) & 1))
    for f in range(FIELDS):
        block = wide[f * 8:f * 8 + 8]
        for half in range(2):
            chosen = jnp.where(inside & ((row & 3) >> 1 == half), block, 0.0)
            reg_buf[f, :, pl.ds(half * 128, 128)] = jnp.sum(chosen, axis=0, keepdims=True)
    reg_copy = pltpu.make_async_copy(reg_buf, reg_out, reg_sem)
    reg_copy.start()
    adv_copy.wait()
    reg_copy.wait()


def solution(mesh):
    n_grp, n_dev = mesh.shape["grp"], mesh.shape["dev"]
    nx = X_CHIPS
    nz = n_grp // nx

    def local(block_states, dest_dev, dest_slot, neighbours, coarse_map):
        blocks = block_states.reshape(SLOTS, FIELDS, 32, 128).transpose(1, 2, 0, 3).reshape(FIELDS, 32 * SLOTS, 128)
        vmem = pl.BlockSpec(memory_space=pltpu.VMEM)
        hbm = pl.BlockSpec(memory_space=pltpu.HBM)
        f32 = jnp.float32
        dma = lambda n: pltpu.SemaphoreType.DMA((n,))
        advanced, sums = pl.pallas_call(
            functools.partial(kernel, nz, nx, n_dev),
            out_shape=(pltpu.VMEM((640, 128), f32), pltpu.VMEM((16, 128), f32)),
            in_specs=[hbm] * 5,
            out_specs=(vmem, vmem),
            scratch_shapes=[
                pltpu.VMEM((FIELDS, 32 * SLOTS, 128), f32), pltpu.SMEM(dest_dev.shape, jnp.int32), pltpu.SMEM(dest_slot.shape, jnp.int32),
                pltpu.SMEM(neighbours.shape, jnp.int32), pltpu.SMEM(coarse_map.shape, jnp.int32),
                pltpu.SMEM((3 * PATCHES,), jnp.int32),
                pltpu.VMEM((SLOTS, EDGE, 128), f32), pltpu.VMEM((SLOTS, EDGE, 128), f32),
                pltpu.VMEM((SLOTS, INNER, 128), f32),
                pltpu.VMEM((SENT, EDGE, 128), f32), pltpu.VMEM((ENTRIES, EDGE, 128), f32),
                pltpu.VMEM((HOPS, INNER, 128), f32), pltpu.VMEM((HOPS, INNER, 128), f32),
                pltpu.VMEM((3 * PATCHES, EDGE, 128), f32), pltpu.VMEM((80, 128), f32), pltpu.VMEM((80, 128), f32),
                pltpu.VMEM((80, 128), f32), pltpu.VMEM((80, 128), f32),
                pltpu.VMEM((480, 128), f32),
                pltpu.VMEM((nx * 16, 128), f32), pltpu.VMEM((nz, 16, 128), f32), pltpu.VMEM((max(nz - 1, 1), 16, 128), f32),
                dma(len(AHEAD)), dma(len(AHEAD)), dma(HOPS), dma(HOPS), dma(2), dma(2),
                dma(max(nx - 1, 1)), dma(max(nx - 1, 1)), dma(max(nz - 1, 1)), dma(max(nz - 1, 1)), dma(7), pltpu.SemaphoreType.REGULAR,
            ],
            compiler_params=pltpu.CompilerParams(collective_id=0, has_side_effects=True, vmem_limit_bytes=24 * 1024 * 1024),
        )(*[pltpu.with_memory_space_constraint(a, pltpu.HBM) for a in (blocks, dest_dev, dest_slot, neighbours, coarse_map)])
        advanced, registers = pl.pallas_call(
            finish,
            out_shape=(jax.ShapeDtypeStruct((640, 128), f32), jax.ShapeDtypeStruct((FIELDS, 1, 256), f32)),
            in_specs=[pl.BlockSpec(memory_space=pl.ANY), vmem],
            out_specs=(hbm, hbm),
            scratch_shapes=[pltpu.VMEM((FIELDS, 1, 256), f32), pltpu.SemaphoreType.DMA, pltpu.SemaphoreType.DMA],
        )(*[pltpu.with_memory_space_constraint(a, pltpu.VMEM) for a in (advanced, sums)])
        advanced = advanced.reshape(FIELDS, 32, PATCHES, 128).transpose(2, 0, 1, 3).reshape(PATCHES, FIELDS, 4096)
        return advanced, registers.transpose(1, 0, 2)

    in_specs = (P(("grp", "dev"), None, None), P("grp"), P("grp"), P(None, "grp"), P("dev", None))
    out_specs = (P(("grp", "dev"), None, None), P(("grp", "dev"), None, None))
    return jax.shard_map(local, mesh=mesh, in_specs=in_specs, out_specs=out_specs, check_vma=False)
```

```python
import functools

import jax
import jax.numpy as jnp
from jax import lax
from jax.experimental import pallas as pl
from jax.experimental.pallas import tpu as pltpu
from jax.sharding import PartitionSpec as P

X_CHIPS = 4
FIELDS = 5
PATCHES = 4
SLOTS = 8
GAMMA = 1.4
COURANT = 0.2
MESH = pl.DeviceIdType.MESH
HIGHEST = lax.Precision.HIGHEST
HOPS = 3

EDGE = 20
INNER = 120

AHEAD = (
    (4, 13, (("low", 3),)),
    (3, 10, (("low", 2), ("low", 3), ("high", 3))),
    (2, 6, (("low", 1), ("low", 2), ("low", 3), ("high", 2))),
    (1, 0, (("kept", 1), ("kept", 2), ("kept", 3), ("low", 1), ("low", 2), ("high", 1))),
    (-1, 14, (("kept", 0), ("kept", 1), ("kept", 2))),
)
SENT = 17
OWN = SENT
ENTRIES = SENT + PATCHES + 1
LOW_AT = ((None, 6, 10, 13), (None, 3, 7, 11), (None, OWN + PATCHES, 4, 8))
LOW_KEPT = (-1, OWN, 14)
HIGH_AT = (None, 5, 9, 12)


def primitives(u):
    inverse = 1.0 / u[0]
    vx, vy, vz = u[1] * inverse, u[2] * inverse, u[3] * inverse
    kinetic = 0.5 * (u[1] * vx + u[2] * vy + u[3] * vz)
    return [u[0], vx, vy, vz, (GAMMA - 1.0) * (u[4] - kinetic)]


def half_slopes(below, centre, above):
    out = []
    for b, c, a in zip(below, centre, above):
        down, up = c - b, a - c
        slope = jnp.maximum(0.0, jnp.minimum(down, up)) + jnp.minimum(0.0, jnp.maximum(down, up))
        out.append(0.5 * slope)
    return out


def euler_flux(prim):
    r, vx, vy, vz, p = prim
    mass = r * vx
    energy = p * (1.0 / (GAMMA - 1.0)) + 0.5 * r * (vx * vx + vy * vy + vz * vz)
    flux = [mass, mass * vx + p, mass * vy, mass * vz, vx * (energy + p)]
    cons = [r, mass, r * vy, r * vz, energy]
    return flux, cons, jnp.abs(vx) + jnp.sqrt(GAMMA * p / r)


def interface(left_prim, left_half, right_prim, right_half):
    left = [c + s for c, s in zip(left_prim, left_half)]
    right = [c - s for c, s in zip(right_prim, right_half)]
    lf, lc, ls = euler_flux(left)
    rf, rc, rs = euler_flux(right)
    largest = 0.5 * jnp.maximum(ls, rs)
    return [0.5 * (a + b) - largest * (d - c) for a, b, c, d in zip(lf, rf, lc, rc)]


def iota(shape, dim):
    return lax.broadcasted_iota(jnp.int32, shape, dim)


def kernel(
    nz, nx, n_dev,
    blk_hbm, ddev_hbm, dslot_hbm, nbr_hbm, cmap_hbm,
    adv, sums,
    blk, ddev, dslot, nbr, cmap, table,
    slot_low, slot_high, slot_inner, edge_send, edges, inner_send, inner_recv, near, low, high, lower, upper, inner,
    xpool, zbuf, zrecv,
    edge_ss, edge_rs, inner_ss, inner_rs, ghost_ss, ghost_rs, x_ss, x_rs, z_ss, z_rs, in_sem, ready,
):
    me = lax.axis_index("dev")
    grp = lax.axis_index("grp")
    mz, mx = grp >> (nx.bit_length() - 1), grp & (nx - 1)
    dev_of = lambda place: place & (n_dev - 1)
    z_of = lambda by: jnp.where(mz + by >= nz, mz + (by - nz), mz + by)
    dev_at = lambda by: (grp, dev_of(me + by))
    x_at = lambda by: ((grp - mx) + ((mx + by) & (nx - 1)), me)
    z_at = lambda by: (z_of(by) * nx + mx, me)

    barrier = pltpu.get_barrier_semaphore()
    for by in (-1, 1, -2, -3, -4):
        pl.semaphore_signal(barrier, inc=1, device_id=dev_at(by), device_id_type=MESH)
    for by in range(1, nx):
        pl.semaphore_signal(barrier, inc=1, device_id=x_at(by), device_id_type=MESH)
    loads = []
    top, bottom, middle = pl.ds(28 * SLOTS, 4 * SLOTS), pl.ds(0, 4 * SLOTS), pl.ds(4 * SLOTS, 24 * SLOTS)
    for n, (source, held) in enumerate((
        (ddev_hbm, ddev), (dslot_hbm, dslot),
        (blk_hbm.at[:, bottom], blk.at[:, bottom]), (blk_hbm.at[:, top], blk.at[:, top]),
        (nbr_hbm, nbr), (cmap_hbm, cmap), (blk_hbm.at[:, middle], blk.at[:, middle]))):
        copy = pltpu.make_async_copy(source, held, in_sem.at[n])
        copy.start()
        loads.append(copy)
    for by in range(1, nz):
        @pl.when(mz + by < nz)
        def _():
            pl.semaphore_signal(barrier, inc=1, device_id=z_at(by), device_id_type=MESH)

    loads[0].wait()
    loads[1].wait()
    going = [None]
    for k in range(1, HOPS + 1):
        target = dev_of(me + k)
        slot = jnp.int32(0)
        for j in range(SLOTS):
            slot = jnp.where(ddev[me * SLOTS + j] == target, j, slot)
        going.append(slot)
    own_slot = []
    for q in range(PATCHES):
        slot = jnp.int32(0)
        for j in range(SLOTS):
            i = me * SLOTS + j
            slot = jnp.where((ddev[i] == me) & (dslot[i] == q), j, slot)
        own_slot.append(slot)

    loads[2].wait()
    loads[3].wait()
    for j in range(SLOTS):
        for f in range(FIELDS):
            slot_low[j, pl.ds(f * 4, 4), :] = blk[f, pl.ds(j, 4, stride=SLOTS), :]
            slot_high[j, pl.ds(f * 4, 4), :] = blk[f, pl.ds(28 * SLOTS + j, 4, stride=SLOTS), :]
    for _, first, entries in AHEAD:
        for n, (what, j) in enumerate(entries):
            if what == "high":
                edge_send[first + n] = slot_high[going[j]]
            else:
                edge_send[first + n] = slot_low[own_slot[j] if what == "kept" else going[j]]

    pl.semaphore_wait(barrier, 5 + (nx - 1) + mz)

    edge_copies = []
    for n, (by, first, entries) in enumerate(AHEAD):
        part = pl.ds(first, len(entries))
        copy = pltpu.make_async_remote_copy(
            src_ref=edge_send.at[part], dst_ref=edges.at[part],
            send_sem=edge_ss.at[n], recv_sem=edge_rs.at[n], device_id=dev_at(by), device_id_type=MESH)
        copy.start()
        edge_copies.append(copy)

    for by in range(1, nz):
        @pl.when(mz >= by)
        def _():
            pl.semaphore_signal(ready, inc=1, device_id=z_at(nz - by), device_id_type=MESH)

    for q in range(PATCHES):
        edges[OWN + q] = slot_low[own_slot[q]]
    edges[OWN + PATCHES] = slot_low[going[1]]
    origin = [jnp.int32(0)] * PATCHES
    high_at = [jnp.int32(0)] * PATCHES
    low_at = []
    for beside in range(3):
        place = dev_of(me + beside - 1)
        at = [jnp.int32(min(max(LOW_KEPT[beside] + q, 0), ENTRIES - 1)) for q in range(PATCHES)]
        for k in range(1, HOPS + 1):
            source = dev_of(place - k)
            landing = jnp.int32(-1)
            for j in range(SLOTS):
                i = source * SLOTS + j
                landing = jnp.where(ddev[i] == place, dslot[i], landing)
            for q in range(PATCHES):
                at[q] = jnp.where(landing == q, LOW_AT[beside][k], at[q])
                if beside == 1:
                    origin[q] = jnp.where(landing == q, k, origin[q])
                    high_at[q] = jnp.where(landing == q, HIGH_AT[k], high_at[q])
        for q in range(PATCHES):
            table[beside * PATCHES + q] = at[q]
        low_at.append(at)
    loads[4].wait()
    lower_nbr = [nbr[0, me * PATCHES + q] for q in range(PATCHES)]
    upper_nbr = [nbr[1, me * PATCHES + q] for q in range(PATCHES)]

    def place_of(nb, q):
        place = jnp.where(nb < 0, PATCHES + q, nb - (me - 1) * PATCHES)
        return jnp.minimum(jnp.maximum(place, 0), 3 * PATCHES - 1)

    above_at = [table[place_of(upper_nbr[q], q)] for q in range(PATCHES)]
    patch = iota((8, 128), 0) & 3
    lower_ids = jnp.zeros((8, 128), jnp.int32)
    upper_ids = jnp.zeros((8, 128), jnp.int32)
    for q in range(PATCHES):
        lower_ids = jnp.where(patch == q, lower_nbr[q], lower_ids)
        upper_ids = jnp.where(patch == q, upper_nbr[q], upper_ids)
    loads[5].wait()

    width = 8 * nx
    column = iota((8, 4 * width), 1)
    target = jnp.zeros((8, 4 * width), jnp.int32)
    for i in range(nx):
        source = (grp - mx) + ((mx - i) & (nx - 1))
        for q in range(PATCHES):
            at = (((column & (width - 1)) >> 3) == i) & ((column & 3) == q)
            target = jnp.where(at, cmap[0, source * PATCHES + q], target)
    row8 = iota((8, width), 0)
    same_half = (row8 >> 2) == ((iota((8, width), 1) >> 2) & 1)
    route = []
    for i in range(nz):
        code = (z_of(i) * nx + mx) * PATCHES
        route.append(jnp.where((target[:, :width] == code + (row8 & 3)) & same_half, 1.0, 0.0))
    route = jnp.concatenate(route, axis=0)
    wide_row, wide_column = iota((2 * nz, 4 * width), 0), iota((2 * nz, 4 * width), 1)
    place_z = mz + (wide_row >> 1)
    place_z = jnp.where(place_z >= nz, place_z - nz, place_z)
    code = (place_z * nx + mx) * PATCHES + sum((wide_column >= t * width).astype(jnp.int32) for t in range(1, 4))
    wide_target = jnp.broadcast_to(target[0:1], (2 * nz, 4 * width))
    wide_route = jnp.where((wide_target == code) & ((wide_row & 1) == ((wide_column >> 2) & 1)), 1.0, 0.0)

    for copy in edge_copies:
        copy.wait_recv()
    for q in range(PATCHES):
        edge = jnp.where(origin[q] > 0, edges[high_at[q]], slot_high[own_slot[q]])
        near[PATCHES + q] = edge
        high[pl.ds(q, EDGE, stride=PATCHES), :] = edge
        upper[pl.ds(q, EDGE, stride=PATCHES), :] = edges[above_at[q]]

    def outer(side, layer):
        return [side[pl.ds(f * 16 + layer * 8, 8), :] for f in range(FIELDS)]

    last = outer(high, 1)
    ghosts_above = [
        [jnp.where(upper_ids < 0, a, b) for a, b in zip(last, outer(upper, layer))] for layer in range(2)]
    p14 = primitives(outer(high, 0))
    p15 = primitives(last)
    p16 = primitives(ghosts_above[0])
    p17 = primitives(ghosts_above[1])
    s15 = half_slopes(p14, p15, p16)
    s16 = half_slopes(p15, p16, p17)
    top_flux = interface(p15, s15, p16, s16)

    lane_in, lane_out = iota((128, 128), 0), iota((128, 128), 1)
    mean = jnp.where(
        (lane_in >> 5 == (lane_out >> 3) & 3) & ((lane_in & 15) >> 1 == (lane_out & 7)), 0.25, 0.0)
    coarse = jnp.dot(jnp.concatenate(top_flux, axis=0), mean, precision=HIGHEST, preferred_element_type=jnp.float32)
    lane8 = iota((8, 128), 1)
    packed = coarse[0:8]
    for f in range(1, 4):
        packed = jnp.where(lane8 >> 5 == f, coarse[f * 8:f * 8 + 8], packed)
    xpool[0:8, :] = packed
    xpool[8:16, :] = coarse[32:40]
    x_copies = []
    for i in sorted(range(1, nx), key=lambda i: -min(i, nx - i)):
        copy = pltpu.make_async_remote_copy(
            src_ref=xpool.at[pl.ds(0, 16)], dst_ref=xpool.at[pl.ds(i * 16, 16)],
            send_sem=x_ss.at[i - 1], recv_sem=x_rs.at[i - 1], device_id=x_at(i), device_id_type=MESH)
        copy.start()
        x_copies.append(copy)

    for copy in x_copies:
        copy.wait_recv()
    pool = jnp.concatenate([xpool[i * 16:i * 16 + 8, :] for i in range(nx)], axis=0)
    routed = jnp.dot(route, pool, precision=HIGHEST, preferred_element_type=jnp.float32)
    pool = jnp.concatenate([xpool[i * 16 + 8:i * 16 + 16, :] for i in range(nx)], axis=0)
    group = iota((width, 128), 1) >> 5
    pool = jnp.concatenate([jnp.where(group == t, pool, 0.0) for t in range(4)], axis=0)
    routed_fifth = jnp.dot(wide_route, pool, precision=HIGHEST, preferred_element_type=jnp.float32)
    for i in range(nz):
        zbuf[i, 0:8, :] = routed[i * 8:i * 8 + 8]
        zbuf[i, 8:10, :] = routed_fifth[i * 2:i * 2 + 2]
    z_copies = []
    for i in range(1, nz):
        copy = pltpu.make_async_remote_copy(
            src_ref=zbuf.at[i, pl.ds(0, 10)], dst_ref=zrecv.at[i - 1, pl.ds(0, 10)],
            send_sem=z_ss.at[i - 1], recv_sem=z_rs.at[i - 1], device_id=z_at(i), device_id_type=MESH)
        pl.when(mz + i >= nz)(copy.start)
        z_copies.append((i, copy))

    ghost_copies = []
    for n, (by, first, to) in enumerate(((1, 1, 1), (-1, 0, 2 * PATCHES))):
        copy = pltpu.make_async_remote_copy(
            src_ref=near.at[pl.ds(PATCHES + first, 3)], dst_ref=near.at[pl.ds(to, 3)],
            send_sem=ghost_ss.at[n], recv_sem=ghost_rs.at[n], device_id=dev_at(by), device_id_type=MESH)
        copy.start()
        ghost_copies.append(copy)
    loads[6].wait()
    for j in range(SLOTS):
        for f in range(FIELDS):
            slot_inner[j, pl.ds(f * 24, 24), :] = blk[f, pl.ds(4 * SLOTS + j, 24, stride=SLOTS), :]
    inner_copies = []
    for k in range(HOPS):
        inner_send[k] = slot_inner[going[k + 1]]
        copy = pltpu.make_async_remote_copy(
            src_ref=inner_send.at[k], dst_ref=inner_recv.at[k],
            send_sem=inner_ss.at[k], recv_sem=inner_rs.at[k], device_id=dev_at(k + 1), device_id_type=MESH)
        copy.start()
        inner_copies.append(copy)

    for copy in ghost_copies:
        copy.wait_recv()
    for q in range(PATCHES):
        low[pl.ds(q, EDGE, stride=PATCHES), :] = edges[low_at[1][q]]
        lower[pl.ds(q, EDGE, stride=PATCHES), :] = near[place_of(lower_nbr[q], q)]
    for copy in inner_copies:
        copy.wait_recv()
    for q in range(PATCHES):
        arrived = jnp.maximum(origin[q] - 1, 0)
        for f in range(FIELDS):
            mine = slot_inner[own_slot[q], pl.ds(f * 24, 24), :]
            theirs = inner_recv[arrived, pl.ds(f * 24, 24), :]
            inner[pl.ds(f * 96 + q, 24, stride=PATCHES), :] = jnp.where(origin[q] > 0, theirs, mine)

    first = outer(low, 0)
    ghosts_below = [
        [jnp.where(lower_ids < 0, a, b) for a, b in zip(first, outer(lower, layer))] for layer in range(2)]

    def layer(x):
        if x < 2:
            return outer(low, x)
        if x >= 14:
            return outer(high, x - 14)
        return [inner[pl.ds(f * 96 + (x - 2) * 8, 8), :] for f in range(FIELDS)]

    here, above = primitives(ghosts_below[1]), primitives(first)
    slope = half_slopes(primitives(ghosts_below[0]), here, above)
    below_flux = None
    for x in range(17):
        beyond = p17 if x == 16 else p16 if x == 15 else primitives(layer(x + 1))
        slope_above = half_slopes(here, above, beyond)
        flux = top_flux if x == 16 else interface(here, slope, above, slope_above)
        if x > 0:
            u = layer(x - 1)
            for f in range(FIELDS):
                adv[pl.ds(f * 128 + (x - 1) * 8, 8), :] = u[f] - COURANT * (flux[f] - below_flux[f])
        here, above, slope, below_flux = above, beyond, slope_above, flux

    @pl.when(mz < nz - 1)
    def _():
        pl.semaphore_wait(ready, nz - 1 - mz)
        for i, copy in z_copies:
            pl.when(mz + i < nz)(copy.start)
    z_copies = [copy for _, copy in z_copies]
    for copy in z_copies:
        copy.wait_recv()
    total, fifth = zbuf[0, 0:8, :], zbuf[0, 8:10, :]
    for i in range(nz - 1):
        total = total + zrecv[i, 0:8, :]
        fifth = fifth + zrecv[i, 8:10, :]
    sums[0:8, :] = total
    sums[8:10, :] = fifth

    for copy in edge_copies + ghost_copies + inner_copies + x_copies + z_copies:
        copy.wait_send()


def finish(adv, sums, adv_out, reg_out, reg_buf, adv_sem, reg_sem):
    adv_copy = pltpu.make_async_copy(adv, adv_out, adv_sem)
    adv_copy.start()
    lane_in, lane_out = iota((128, 128), 0), iota((128, 128), 1)
    lane8 = iota((8, 128), 1)
    total, fifth = sums[0:8, :], sums[8:10, :]
    row = iota((8, 128), 0)
    fifth = jnp.where(row < 4, fifth[0:1], fifth[1:2])
    parts = [jnp.where(lane8 >> 5 == f, total, 0.0) for f in range(4)]
    parts.append(jnp.where(lane8 >> 5 == row & 3, fifth, 0.0))
    place = jnp.where(
        (lane_in & 31) == ((lane_out >> 4) & 3) * 8 + (lane_out & 7), 1.0, 0.0)
    wide = jnp.dot(jnp.concatenate(parts, axis=0), place, precision=HIGHEST, preferred_element_type=jnp.float32)
    inside = (row >> 2 == lane8 >> 6) & ((row & 1) == ((lane8 >> 3) & 1))
    for f in range(FIELDS):
        block = wide[f * 8:f * 8 + 8]
        for half in range(2):
            chosen = jnp.where(inside & ((row & 3) >> 1 == half), block, 0.0)
            reg_buf[f, :, pl.ds(half * 128, 128)] = jnp.sum(chosen, axis=0, keepdims=True)
    reg_copy = pltpu.make_async_copy(reg_buf, reg_out, reg_sem)
    reg_copy.start()
    adv_copy.wait()
    reg_copy.wait()


def solution(mesh):
    n_grp, n_dev = mesh.shape["grp"], mesh.shape["dev"]
    nx = X_CHIPS
    nz = n_grp // nx

    def local(block_states, dest_dev, dest_slot, neighbours, coarse_map):
        blocks = block_states.reshape(SLOTS, FIELDS, 32, 128).transpose(1, 2, 0, 3).reshape(FIELDS, 32 * SLOTS, 128)
        vmem = pl.BlockSpec(memory_space=pltpu.VMEM)
        hbm = pl.BlockSpec(memory_space=pltpu.HBM)
        f32 = jnp.float32
        dma = lambda n: pltpu.SemaphoreType.DMA((n,))
        advanced, sums = pl.pallas_call(
            functools.partial(kernel, nz, nx, n_dev),
            out_shape=(pltpu.VMEM((640, 128), f32), pltpu.VMEM((16, 128), f32)),
            in_specs=[hbm] * 5,
            out_specs=(vmem, vmem),
            scratch_shapes=[
                pltpu.VMEM((FIELDS, 37 * SLOTS, 128), f32), pltpu.SMEM(dest_dev.shape, jnp.int32), pltpu.SMEM(dest_slot.shape, jnp.int32),
                pltpu.SMEM(neighbours.shape, jnp.int32), pltpu.SMEM(coarse_map.shape, jnp.int32),
                pltpu.SMEM((3 * PATCHES,), jnp.int32),
                pltpu.VMEM((SLOTS, EDGE, 128), f32), pltpu.VMEM((SLOTS, EDGE, 128), f32),
                pltpu.VMEM((SLOTS, INNER, 128), f32),
                pltpu.VMEM((SENT, EDGE, 128), f32), pltpu.VMEM((ENTRIES, EDGE, 128), f32),
                pltpu.VMEM((HOPS, INNER, 128), f32), pltpu.VMEM((HOPS, INNER, 128), f32),
                pltpu.VMEM((3 * PATCHES, EDGE, 128), f32), pltpu.VMEM((104, 128), f32), pltpu.VMEM((104, 128), f32),
                pltpu.VMEM((104, 128), f32), pltpu.VMEM((104, 128), f32),
                pltpu.VMEM((488, 128), f32),
                pltpu.VMEM((nx * 16, 128), f32), pltpu.VMEM((nz, 16, 128), f32), pltpu.VMEM((max(nz - 1, 1), 16, 128), f32),
                dma(len(AHEAD)), dma(len(AHEAD)), dma(HOPS), dma(HOPS), dma(2), dma(2),
                dma(max(nx - 1, 1)), dma(max(nx - 1, 1)), dma(max(nz - 1, 1)), dma(max(nz - 1, 1)), dma(7), pltpu.SemaphoreType.REGULAR,
            ],
            compiler_params=pltpu.CompilerParams(collective_id=0, has_side_effects=True, vmem_limit_bytes=24 * 1024 * 1024),
        )(*[pltpu.with_memory_space_constraint(a, pltpu.HBM) for a in (blocks, dest_dev, dest_slot, neighbours, coarse_map)])
        advanced, registers = pl.pallas_call(
            finish,
            out_shape=(jax.ShapeDtypeStruct((640, 128), f32), jax.ShapeDtypeStruct((FIELDS, 1, 256), f32)),
            in_specs=[pl.BlockSpec(memory_space=pl.ANY), vmem],
            out_specs=(hbm, hbm),
            scratch_shapes=[pltpu.VMEM((FIELDS, 1, 256), f32), pltpu.SemaphoreType.DMA, pltpu.SemaphoreType.DMA],
        )(*[pltpu.with_memory_space_constraint(a, pltpu.VMEM) for a in (advanced, sums)])
        advanced = advanced.reshape(FIELDS, 32, PATCHES, 128).transpose(2, 0, 1, 3).reshape(PATCHES, FIELDS, 4096)
        return advanced, registers.transpose(1, 0, 2)

    in_specs = (P(("grp", "dev"), None, None), P("grp"), P("grp"), P(None, "grp"), P("dev", None))
    out_specs = (P(("grp", "dev"), None, None), P(("grp", "dev"), None, None))
    return jax.shard_map(local, mesh=mesh, in_specs=in_specs, out_specs=out_specs, check_vma=False)
```

```python
import functools

import jax
import jax.numpy as jnp
from jax import lax
from jax.experimental import pallas as pl
from jax.experimental.pallas import tpu as pltpu
from jax.sharding import PartitionSpec as P

X_CHIPS = 4
FIELDS = 5
PATCHES = 4
SLOTS = 8
GAMMA = 1.4
COURANT = 0.2
MESH = pl.DeviceIdType.MESH
HIGHEST = lax.Precision.HIGHEST
HOPS = 3

EDGE = 20
INNER = 120

AHEAD = (
    (-1, 14, (("kept", 0), ("kept", 1), ("kept", 2))),
    (4, 13, (("low", 3),)),
    (3, 10, (("low", 2), ("low", 3), ("high", 3))),
    (2, 6, (("low", 1), ("low", 2), ("low", 3), ("high", 2))),
    (1, 0, (("kept", 1), ("kept", 2), ("kept", 3), ("low", 1), ("low", 2), ("high", 1))),
)
SENT = 17
OWN = SENT
ENTRIES = SENT + PATCHES + 1
LOW_AT = ((None, 6, 10, 13), (None, 3, 7, 11), (None, OWN + PATCHES, 4, 8))
LOW_KEPT = (-1, OWN, 14)
HIGH_AT = (None, 5, 9, 12)


def primitives(u):
    inverse = 1.0 / u[0]
    vx, vy, vz = u[1] * inverse, u[2] * inverse, u[3] * inverse
    kinetic = 0.5 * (u[1] * vx + u[2] * vy + u[3] * vz)
    return [u[0], vx, vy, vz, (GAMMA - 1.0) * (u[4] - kinetic)]


def half_slopes(below, centre, above):
    out = []
    for b, c, a in zip(below, centre, above):
        down, up = c - b, a - c
        slope = jnp.maximum(0.0, jnp.minimum(down, up)) + jnp.minimum(0.0, jnp.maximum(down, up))
        out.append(0.5 * slope)
    return out


def euler_flux(prim):
    r, vx, vy, vz, p = prim
    mass = r * vx
    energy = p * (1.0 / (GAMMA - 1.0)) + 0.5 * r * (vx * vx + vy * vy + vz * vz)
    flux = [mass, mass * vx + p, mass * vy, mass * vz, vx * (energy + p)]
    cons = [r, mass, r * vy, r * vz, energy]
    return flux, cons, jnp.abs(vx) + jnp.sqrt(GAMMA * p / r)


def interface(left_prim, left_half, right_prim, right_half):
    left = [c + s for c, s in zip(left_prim, left_half)]
    right = [c - s for c, s in zip(right_prim, right_half)]
    lf, lc, ls = euler_flux(left)
    rf, rc, rs = euler_flux(right)
    largest = 0.5 * jnp.maximum(ls, rs)
    return [0.5 * (a + b) - largest * (d - c) for a, b, c, d in zip(lf, rf, lc, rc)]


def iota(shape, dim):
    return lax.broadcasted_iota(jnp.int32, shape, dim)


def kernel(
    nz, nx, n_dev,
    blk_hbm, ddev_hbm, dslot_hbm, nbr_hbm, cmap_hbm,
    adv, sums,
    blk, ddev, dslot, nbr, cmap, table,
    slot_low, slot_high, slot_inner, edge_send, edges, inner_send, inner_recv, near, low, high, lower, upper, inner,
    xpool, zbuf, zrecv,
    edge_ss, edge_rs, inner_ss, inner_rs, ghost_ss, ghost_rs, x_ss, x_rs, z_ss, z_rs, in_sem, ready,
):
    me = lax.axis_index("dev")
    grp = lax.axis_index("grp")
    mz, mx = grp >> (nx.bit_length() - 1), grp & (nx - 1)
    dev_of = lambda place: place & (n_dev - 1)
    z_of = lambda by: jnp.where(mz + by >= nz, mz + (by - nz), mz + by)
    dev_at = lambda by: (grp, dev_of(me + by))
    x_at = lambda by: ((grp - mx) + ((mx + by) & (nx - 1)), me)
    z_at = lambda by: (z_of(by) * nx + mx, me)

    barrier = pltpu.get_barrier_semaphore()
    for by in (-1, 1, -2, -3, -4):
        pl.semaphore_signal(barrier, inc=1, device_id=dev_at(by), device_id_type=MESH)
    for by in range(1, nx):
        pl.semaphore_signal(barrier, inc=1, device_id=x_at(by), device_id_type=MESH)
    loads = []
    top, bottom, middle = pl.ds(28 * SLOTS, 4 * SLOTS), pl.ds(0, 4 * SLOTS), pl.ds(4 * SLOTS, 24 * SLOTS)
    for n, (source, held) in enumerate((
        (ddev_hbm, ddev), (dslot_hbm, dslot),
        (blk_hbm.at[:, bottom], blk.at[:, bottom]), (blk_hbm.at[:, top], blk.at[:, top]),
        (nbr_hbm, nbr), (cmap_hbm, cmap), (blk_hbm.at[:, middle], blk.at[:, middle]))):
        copy = pltpu.make_async_copy(source, held, in_sem.at[n])
        copy.start()
        loads.append(copy)
    for by in range(1, nz):
        @pl.when(mz + by < nz)
        def _():
            pl.semaphore_signal(barrier, inc=1, device_id=z_at(by), device_id_type=MESH)

    loads[0].wait()
    loads[1].wait()
    going = [None]
    for k in range(1, HOPS + 1):
        target = dev_of(me + k)
        slot = jnp.int32(0)
        for j in range(SLOTS):
            slot = jnp.where(ddev[me * SLOTS + j] == target, j, slot)
        going.append(slot)
    own_slot = []
    for q in range(PATCHES):
        slot = jnp.int32(0)
        for j in range(SLOTS):
            i = me * SLOTS + j
            slot = jnp.where((ddev[i] == me) & (dslot[i] == q), j, slot)
        own_slot.append(slot)

    loads[2].wait()
    loads[3].wait()
    for j in range(SLOTS):
        for f in range(FIELDS):
            slot_low[j, pl.ds(f * 4, 4), :] = blk[f, pl.ds(j, 4, stride=SLOTS), :]
            slot_high[j, pl.ds(f * 4, 4), :] = blk[f, pl.ds(28 * SLOTS + j, 4, stride=SLOTS), :]
    for _, first, entries in AHEAD:
        for n, (what, j) in enumerate(entries):
            if what == "high":
                edge_send[first + n] = slot_high[going[j]]
            else:
                edge_send[first + n] = slot_low[own_slot[j] if what == "kept" else going[j]]

    pl.semaphore_wait(barrier, 5 + (nx - 1) + mz)

    edge_copies = []
    for n, (by, first, entries) in enumerate(AHEAD):
        part = pl.ds(first, len(entries))
        copy = pltpu.make_async_remote_copy(
            src_ref=edge_send.at[part], dst_ref=edges.at[part],
            send_sem=edge_ss.at[n], recv_sem=edge_rs.at[n], device_id=dev_at(by), device_id_type=MESH)
        copy.start()
        edge_copies.append(copy)

    for by in range(1, nz):
        @pl.when(mz >= by)
        def _():
            pl.semaphore_signal(ready, inc=1, device_id=z_at(nz - by), device_id_type=MESH)

    for q in range(PATCHES):
        edges[OWN + q] = slot_low[own_slot[q]]
    edges[OWN + PATCHES] = slot_low[going[1]]
    origin = [jnp.int32(0)] * PATCHES
    high_at = [jnp.int32(0)] * PATCHES
    low_at = []
    for beside in range(3):
        place = dev_of(me + beside - 1)
        at = [jnp.int32(min(max(LOW_KEPT[beside] + q, 0), ENTRIES - 1)) for q in range(PATCHES)]
        for k in range(1, HOPS + 1):
            source = dev_of(place - k)
            landing = jnp.int32(-1)
            for j in range(SLOTS):
                i = source * SLOTS + j
                landing = jnp.where(ddev[i] == place, dslot[i], landing)
            for q in range(PATCHES):
                at[q] = jnp.where(landing == q, LOW_AT[beside][k], at[q])
                if beside == 1:
                    origin[q] = jnp.where(landing == q, k, origin[q])
                    high_at[q] = jnp.where(landing == q, HIGH_AT[k], high_at[q])
        for q in range(PATCHES):
            table[beside * PATCHES + q] = at[q]
        low_at.append(at)
    loads[4].wait()
    lower_nbr = [nbr[0, me * PATCHES + q] for q in range(PATCHES)]
    upper_nbr = [nbr[1, me * PATCHES + q] for q in range(PATCHES)]

    def place_of(nb, q):
        place = jnp.where(nb < 0, PATCHES + q, nb - (me - 1) * PATCHES)
        return jnp.minimum(jnp.maximum(place, 0), 3 * PATCHES - 1)

    above_at = [table[place_of(upper_nbr[q], q)] for q in range(PATCHES)]
    patch = iota((8, 128), 0) & 3
    lower_ids = jnp.zeros((8, 128), jnp.int32)
    upper_ids = jnp.zeros((8, 128), jnp.int32)
    for q in range(PATCHES):
        lower_ids = jnp.where(patch == q, lower_nbr[q], lower_ids)
        upper_ids = jnp.where(patch == q, upper_nbr[q], upper_ids)
    loads[5].wait()

    width = 8 * nx
    column = iota((8, 4 * width), 1)
    target = jnp.zeros((8, 4 * width), jnp.int32)
    for i in range(nx):
        source = (grp - mx) + ((mx - i) & (nx - 1))
        for q in range(PATCHES):
            at = (((column & (width - 1)) >> 3) == i) & ((column & 3) == q)
            target = jnp.where(at, cmap[0, source * PATCHES + q], target)
    row8 = iota((8, width), 0)
    same_half = (row8 >> 2) == ((iota((8, width), 1) >> 2) & 1)
    route = []
    for i in range(nz):
        code = (z_of(i) * nx + mx) * PATCHES
        route.append(jnp.where((target[:, :width] == code + (row8 & 3)) & same_half, 1.0, 0.0))
    route = jnp.concatenate(route, axis=0)
    wide_row, wide_column = iota((2 * nz, 4 * width), 0), iota((2 * nz, 4 * width), 1)
    place_z = mz + (wide_row >> 1)
    place_z = jnp.where(place_z >= nz, place_z - nz, place_z)
    code = (place_z * nx + mx) * PATCHES + sum((wide_column >= t * width).astype(jnp.int32) for t in range(1, 4))
    wide_target = jnp.broadcast_to(target[0:1], (2 * nz, 4 * width))
    wide_route = jnp.where((wide_target == code) & ((wide_row & 1) == ((wide_column >> 2) & 1)), 1.0, 0.0)

    for copy in edge_copies:
        copy.wait_recv()
    for q in range(PATCHES):
        edge = jnp.where(origin[q] > 0, edges[high_at[q]], slot_high[own_slot[q]])
        near[PATCHES + q] = edge
        high[pl.ds(q, EDGE, stride=PATCHES), :] = edge
        upper[pl.ds(q, EDGE, stride=PATCHES), :] = edges[above_at[q]]

    def outer(side, layer):
        return [side[pl.ds(f * 16 + layer * 8, 8), :] for f in range(FIELDS)]

    last = outer(high, 1)
    ghosts_above = [
        [jnp.where(upper_ids < 0, a, b) for a, b in zip(last, outer(upper, layer))] for layer in range(2)]
    p14 = primitives(outer(high, 0))
    p15 = primitives(last)
    p16 = primitives(ghosts_above[0])
    p17 = primitives(ghosts_above[1])
    s15 = half_slopes(p14, p15, p16)
    s16 = half_slopes(p15, p16, p17)
    top_flux = interface(p15, s15, p16, s16)

    lane_in, lane_out = iota((128, 128), 0), iota((128, 128), 1)
    mean = jnp.where(
        (lane_in >> 5 == (lane_out >> 3) & 3) & ((lane_in & 15) >> 1 == (lane_out & 7)), 0.25, 0.0)
    coarse = jnp.dot(jnp.concatenate(top_flux, axis=0), mean, precision=HIGHEST, preferred_element_type=jnp.float32)
    lane8 = iota((8, 128), 1)
    packed = coarse[0:8]
    for f in range(1, 4):
        packed = jnp.where(lane8 >> 5 == f, coarse[f * 8:f * 8 + 8], packed)
    xpool[0:8, :] = packed
    xpool[8:16, :] = coarse[32:40]
    x_copies = []
    for i in sorted(range(1, nx), key=lambda i: -min(i, nx - i)):
        copy = pltpu.make_async_remote_copy(
            src_ref=xpool.at[pl.ds(0, 16)], dst_ref=xpool.at[pl.ds(i * 16, 16)],
            send_sem=x_ss.at[i - 1], recv_sem=x_rs.at[i - 1], device_id=x_at(i), device_id_type=MESH)
        copy.start()
        x_copies.append(copy)

    for copy in x_copies:
        copy.wait_recv()
    pool = jnp.concatenate([xpool[i * 16:i * 16 + 8, :] for i in range(nx)], axis=0)
    routed = jnp.dot(route, pool, precision=HIGHEST, preferred_element_type=jnp.float32)
    pool = jnp.concatenate([xpool[i * 16 + 8:i * 16 + 16, :] for i in range(nx)], axis=0)
    group = iota((width, 128), 1) >> 5
    pool = jnp.concatenate([jnp.where(group == t, pool, 0.0) for t in range(4)], axis=0)
    routed_fifth = jnp.dot(wide_route, pool, precision=HIGHEST, preferred_element_type=jnp.float32)
    for i in range(nz):
        zbuf[i, 0:8, :] = routed[i * 8:i * 8 + 8]
        zbuf[i, 8:10, :] = routed_fifth[i * 2:i * 2 + 2]
    z_copies = []
    for i in range(1, nz):
        copy = pltpu.make_async_remote_copy(
            src_ref=zbuf.at[i, pl.ds(0, 10)], dst_ref=zrecv.at[i - 1, pl.ds(0, 10)],
            send_sem=z_ss.at[i - 1], recv_sem=z_rs.at[i - 1], device_id=z_at(i), device_id_type=MESH)
        pl.when(mz + i >= nz)(copy.start)
        z_copies.append((i, copy))

    ghost_copies = []
    for n, (by, first, to) in enumerate(((1, 1, 1), (-1, 0, 2 * PATCHES))):
        copy = pltpu.make_async_remote_copy(
            src_ref=near.at[pl.ds(PATCHES + first, 3)], dst_ref=near.at[pl.ds(to, 3)],
            send_sem=ghost_ss.at[n], recv_sem=ghost_rs.at[n], device_id=dev_at(by), device_id_type=MESH)
        copy.start()
        ghost_copies.append(copy)
    loads[6].wait()
    for j in range(SLOTS):
        for f in range(FIELDS):
            slot_inner[j, pl.ds(f * 24, 24), :] = blk[f, pl.ds(4 * SLOTS + j, 24, stride=SLOTS), :]
    inner_copies = []
    for k in range(HOPS):
        inner_send[k] = slot_inner[going[k + 1]]
        copy = pltpu.make_async_remote_copy(
            src_ref=inner_send.at[k], dst_ref=inner_recv.at[k],
            send_sem=inner_ss.at[k], recv_sem=inner_rs.at[k], device_id=dev_at(k + 1), device_id_type=MESH)
        copy.start()
        inner_copies.append(copy)

    for copy in ghost_copies:
        copy.wait_recv()
    for q in range(PATCHES):
        low[pl.ds(q, EDGE, stride=PATCHES), :] = edges[low_at[1][q]]
        lower[pl.ds(q, EDGE, stride=PATCHES), :] = near[place_of(lower_nbr[q], q)]
    for copy in inner_copies:
        copy.wait_recv()
    for q in range(PATCHES):
        arrived = jnp.maximum(origin[q] - 1, 0)
        for f in range(FIELDS):
            mine = slot_inner[own_slot[q], pl.ds(f * 24, 24), :]
            theirs = inner_recv[arrived, pl.ds(f * 24, 24), :]
            inner[pl.ds(f * 96 + q, 24, stride=PATCHES), :] = jnp.where(origin[q] > 0, theirs, mine)

    first = outer(low, 0)
    ghosts_below = [
        [jnp.where(lower_ids < 0, a, b) for a, b in zip(first, outer(lower, layer))] for layer in range(2)]

    def layer(x):
        if x < 2:
            return outer(low, x)
        if x >= 14:
            return outer(high, x - 14)
        return [inner[pl.ds(f * 96 + (x - 2) * 8, 8), :] for f in range(FIELDS)]

    here, above = primitives(ghosts_below[1]), primitives(first)
    slope = half_slopes(primitives(ghosts_below[0]), here, above)
    below_flux = None
    for x in range(17):
        beyond = p17 if x == 16 else p16 if x == 15 else primitives(layer(x + 1))
        slope_above = half_slopes(here, above, beyond)
        flux = top_flux if x == 16 else interface(here, slope, above, slope_above)
        if x > 0:
            u = layer(x - 1)
            for f in range(FIELDS):
                adv[pl.ds(f * 128 + (x - 1) * 8, 8), :] = u[f] - COURANT * (flux[f] - below_flux[f])
        here, above, slope, below_flux = above, beyond, slope_above, flux

    @pl.when(mz < nz - 1)
    def _():
        pl.semaphore_wait(ready, nz - 1 - mz)
        for i, copy in z_copies:
            pl.when(mz + i < nz)(copy.start)
    z_copies = [copy for _, copy in z_copies]
    for copy in z_copies:
        copy.wait_recv()
    total, fifth = zbuf[0, 0:8, :], zbuf[0, 8:10, :]
    for i in range(nz - 1):
        total = total + zrecv[i, 0:8, :]
        fifth = fifth + zrecv[i, 8:10, :]
    sums[0:8, :] = total
    sums[8:10, :] = fifth

    for copy in edge_copies + ghost_copies + inner_copies + x_copies + z_copies:
        copy.wait_send()


def finish(adv, sums, adv_out, reg_out, reg_buf, adv_sem, reg_sem):
    adv_copy = pltpu.make_async_copy(adv, adv_out, adv_sem)
    adv_copy.start()
    lane_in, lane_out = iota((128, 128), 0), iota((128, 128), 1)
    lane8 = iota((8, 128), 1)
    total, fifth = sums[0:8, :], sums[8:10, :]
    row = iota((8, 128), 0)
    fifth = jnp.where(row < 4, fifth[0:1], fifth[1:2])
    parts = [jnp.where(lane8 >> 5 == f, total, 0.0) for f in range(4)]
    parts.append(jnp.where(lane8 >> 5 == row & 3, fifth, 0.0))
    place = jnp.where(
        (lane_in & 31) == ((lane_out >> 4) & 3) * 8 + (lane_out & 7), 1.0, 0.0)
    wide = jnp.dot(jnp.concatenate(parts, axis=0), place, precision=HIGHEST, preferred_element_type=jnp.float32)
    inside = (row >> 2 == lane8 >> 6) & ((row & 1) == ((lane8 >> 3) & 1))
    for f in range(FIELDS):
        block = wide[f * 8:f * 8 + 8]
        for half in range(2):
            chosen = jnp.where(inside & ((row & 3) >> 1 == half), block, 0.0)
            reg_buf[f, :, pl.ds(half * 128, 128)] = jnp.sum(chosen, axis=0, keepdims=True)
    reg_copy = pltpu.make_async_copy(reg_buf, reg_out, reg_sem)
    reg_copy.start()
    adv_copy.wait()
    reg_copy.wait()


def solution(mesh):
    n_grp, n_dev = mesh.shape["grp"], mesh.shape["dev"]
    nx = X_CHIPS
    nz = n_grp // nx

    def local(block_states, dest_dev, dest_slot, neighbours, coarse_map):
        blocks = block_states.reshape(SLOTS, FIELDS, 32, 128).transpose(1, 2, 0, 3).reshape(FIELDS, 32 * SLOTS, 128)
        vmem = pl.BlockSpec(memory_space=pltpu.VMEM)
        hbm = pl.BlockSpec(memory_space=pltpu.HBM)
        f32 = jnp.float32
        dma = lambda n: pltpu.SemaphoreType.DMA((n,))
        advanced, sums = pl.pallas_call(
            functools.partial(kernel, nz, nx, n_dev),
            out_shape=(pltpu.VMEM((640, 128), f32), pltpu.VMEM((16, 128), f32)),
            in_specs=[hbm] * 5,
            out_specs=(vmem, vmem),
            scratch_shapes=[
                pltpu.VMEM((FIELDS, 37 * SLOTS, 128), f32), pltpu.SMEM(dest_dev.shape, jnp.int32), pltpu.SMEM(dest_slot.shape, jnp.int32),
                pltpu.SMEM(neighbours.shape, jnp.int32), pltpu.SMEM(coarse_map.shape, jnp.int32),
                pltpu.SMEM((3 * PATCHES,), jnp.int32),
                pltpu.VMEM((SLOTS, EDGE, 128), f32), pltpu.VMEM((SLOTS, EDGE, 128), f32),
                pltpu.VMEM((SLOTS, INNER, 128), f32),
                pltpu.VMEM((SENT, EDGE, 128), f32), pltpu.VMEM((ENTRIES, EDGE, 128), f32),
                pltpu.VMEM((HOPS, INNER, 128), f32), pltpu.VMEM((HOPS, INNER, 128), f32),
                pltpu.VMEM((3 * PATCHES, EDGE, 128), f32), pltpu.VMEM((104, 128), f32), pltpu.VMEM((104, 128), f32),
                pltpu.VMEM((104, 128), f32), pltpu.VMEM((104, 128), f32),
                pltpu.VMEM((488, 128), f32),
                pltpu.VMEM((nx * 16, 128), f32), pltpu.VMEM((nz, 16, 128), f32), pltpu.VMEM((max(nz - 1, 1), 16, 128), f32),
                dma(len(AHEAD)), dma(len(AHEAD)), dma(HOPS), dma(HOPS), dma(2), dma(2),
                dma(max(nx - 1, 1)), dma(max(nx - 1, 1)), dma(max(nz - 1, 1)), dma(max(nz - 1, 1)), dma(7), pltpu.SemaphoreType.REGULAR,
            ],
            compiler_params=pltpu.CompilerParams(collective_id=0, has_side_effects=True, vmem_limit_bytes=24 * 1024 * 1024),
        )(*[pltpu.with_memory_space_constraint(a, pltpu.HBM) for a in (blocks, dest_dev, dest_slot, neighbours, coarse_map)])
        advanced, registers = pl.pallas_call(
            finish,
            out_shape=(jax.ShapeDtypeStruct((640, 128), f32), jax.ShapeDtypeStruct((FIELDS, 1, 256), f32)),
            in_specs=[pl.BlockSpec(memory_space=pl.ANY), vmem],
            out_specs=(hbm, hbm),
            scratch_shapes=[pltpu.VMEM((FIELDS, 1, 256), f32), pltpu.SemaphoreType.DMA, pltpu.SemaphoreType.DMA],
        )(*[pltpu.with_memory_space_constraint(a, pltpu.VMEM) for a in (advanced, sums)])
        advanced = advanced.reshape(FIELDS, 32, PATCHES, 128).transpose(2, 0, 1, 3).reshape(PATCHES, FIELDS, 4096)
        return advanced, registers.transpose(1, 0, 2)

    in_specs = (P(("grp", "dev"), None, None), P("grp"), P("grp"), P(None, "grp"), P("dev", None))
    out_specs = (P(("grp", "dev"), None, None), P(("grp", "dev"), None, None))
    return jax.shard_map(local, mesh=mesh, in_specs=in_specs, out_specs=out_specs, check_vma=False)
```
